128 devices in a mesh: seq: 16 (over y, x), chan: 8 (over z, core).
Axes of the slice: x: 4, y: 4, z: 4, core: 2. Of those that a mesh axis runs over, the one named last changes fastest.
Arguments:
- gate_out: bfloat16 [16384, 2048], P('seq', 'chan'), may hold values from -6 to 6
- gate_in: bfloat16 [16384, 2048], P('seq', 'chan'), may hold values from -6 to 6
- value_in: bfloat16 [16384, 2048], P('seq', 'chan'), may hold values from -6 to 6
- filter_taps: float32 [16384, 2048], P('seq', 'chan'), may hold values from -1 to 1
- skip_bias: float32 [2048], P('chan'), may hold values from 0.5 to 1.5
- resume_at: int32 [1], replicated, may hold values from 0 to 8191
- out_weight: bfloat16 [2048, 4096], P('chan'), may hold values from -0.1875 to 0.1875
Outputs:
- projected: bfloat16 [16384, 4096], P('seq', 'chan')
The draws below stay inside these ranges and needn't reach their ends.
Inputs may be any that keep to these rules, and one draw needn't show every extreme that they name: `resume_at`: a single position.
All inputs are finite; a program needn't handle non-finite values.
Results may differ from the reference program's by a relative error of at most 0.0049.
Values may be sent and summed in bfloat16 or wider, within the bound.
No kernel may reach another device: no remote copies, remote signals or barrier semaphores. Data moves between devices by JAX's collectives and lax.ppermute only.
A program may use at most 192 MiB of HBM per device.

```python
import math
import jax
import jax.numpy as jnp
from jax import lax

C_DEV = 256
DOUT = 4096
SEQ_LEN = 16384
CHANNELS = 2048


def draw_filter_taps(key, part):
    key = jax.random.fold_in(key, 7)
    keys = jax.random.split(key, 4)
    spans = jnp.exp(jax.random.uniform(keys[0], (CHANNELS,), jnp.float32, math.log(30.0), math.log(4.0 * SEQ_LEN)))
    noise = jnp.clip(jax.random.normal(keys[1], (SEQ_LEN, CHANNELS), jnp.float32), -4.0, 4.0)
    times = jnp.arange(SEQ_LEN, dtype=jnp.int32)[:, None]
    envelope = jnp.exp(-times.astype(jnp.float32) / spans[None, :])
    marks = jax.random.randint(keys[2], (3, CHANNELS), 0, SEQ_LEN)
    falls = jax.random.uniform(keys[3], (3, CHANNELS), jnp.float32, 0.5, 0.8)
    for member in range(3):
        envelope = envelope * jnp.where(times >= marks[member][None, :], falls[member][None, :], 1.0)
    scales = 1.0 / jnp.sqrt(jnp.minimum(spans, float(SEQ_LEN)))
    return (noise * envelope * scales[None, :]).astype(jnp.float32)


def strengthened(array, stream_key, source, target, shards_of, factor):
    def block_of(dim):
        return (jnp.arange(array.shape[dim]) // (array.shape[dim] // shards_of)).reshape((-1,) + (1,) * (array.ndim - 1 - dim))

    first = jax.random.permutation(stream_key, shards_of)[block_of(target)]
    second = (block_of(target) + shards_of // 2) % shards_of
    return jnp.where((block_of(source) == first) | (block_of(source) == second), factor * array, array)


def shard_levels(own_key, shape, shards, least, top_value):
    factor_of, own = 1.0, jax.random.fold_in(own_key, 6)
    for dim, blocks in shards:
        heights = jnp.exp(jax.random.uniform(jax.random.fold_in(own, dim), (blocks,), jnp.float32, least / len(shards), top_value / len(shards)))
        factor_of = factor_of * jnp.repeat(heights, shape[dim] // blocks).reshape([-1 if axis == dim else 1 for axis in range(len(shape))])
    return factor_of


def bell_draw(rng, dims, width, most, cuts=(), held_as=jnp.bfloat16):
    loudness = shard_levels(rng, dims, cuts, -0.22, 0.18) if cuts else 1.0
    result = jax.random.normal(rng, dims, jnp.float32) * width * loudness
    return jnp.minimum(jnp.maximum(result, -most), most).astype(held_as)


def noise_with(rng, shape, spread, most, cuts, heavy, kind=jnp.bfloat16):
    drawn = spread * jax.random.normal(rng, shape, jnp.float32)
    if cuts:
        drawn = drawn * shard_levels(rng, shape, cuts, -0.22, 0.18)
    return jnp.clip(strengthened(drawn, jax.random.fold_in(rng, 3), *heavy), -most, most).astype(kind)


def setup_inputs(seed: int = 0) -> dict:
    splits = jax.random.split(jax.random.key(seed), 8)
    gate_out = bell_draw(splits[0], (SEQ_LEN, CHANNELS), 1.0, 6.0, ((0, 16), (1, 8)))
    gate_in = bell_draw(splits[1], (SEQ_LEN, CHANNELS), 1.0, 6.0, ((0, 16), (1, 8)))
    value_in = bell_draw(splits[2], (SEQ_LEN, CHANNELS), 1.0, 6.0, ((0, 16), (1, 8)))
    filter_taps = draw_filter_taps(jax.random.fold_in(splits[7], 71), 0)
    skip_bias = jnp.clip(0.5 + 1.0 * jax.random.uniform(splits[4], (CHANNELS,), jnp.float32) ** shard_levels(splits[4], (CHANNELS,), ((0, 8),), -0.2, 0.2), 0.5, 1.5)
    resume_at = jax.random.randint(splits[5], (1,), 0, SEQ_LEN // 2).astype(jnp.int32)
    out_weight = noise_with(splits[6], (CHANNELS, DOUT), CHANNELS ** -0.5, 0.1875, ((0, 8),), (0, 1, 8, 2.0))
    return dict(gate_out=gate_out, gate_in=gate_in, value_in=value_in, filter_taps=filter_taps, skip_bias=skip_bias, resume_at=resume_at, out_weight=out_weight)


def causal_block(pair):
    signal_block, taps_block = pair
    seq_rows = signal_block.shape[0]
    period = 2 * seq_rows
    spectrum = jnp.fft.rfft(signal_block, n=period, axis=0) * jnp.fft.rfft(taps_block, n=period, axis=0)
    return jnp.fft.irfft(spectrum, n=period, axis=0)[:seq_rows]


def reference(gate_out, gate_in, value_in, filter_taps, skip_bias, resume_at, out_weight):
    signal = gate_in.astype(jnp.float32) * value_in.astype(jnp.float32)
    seq_rows, channels = signal.shape
    groups = channels // C_DEV
    stacked_signal = jnp.moveaxis(signal.reshape(seq_rows, groups, C_DEV), 1, 0)
    stacked_taps = jnp.moveaxis(filter_taps.reshape(seq_rows, groups, C_DEV), 1, 0)
    convolved = lax.map(causal_block, (stacked_signal, stacked_taps))
    convolved = jnp.moveaxis(convolved, 0, 1).reshape(seq_rows, channels).astype(jnp.float32)
    positions = jnp.arange(seq_rows, dtype=jnp.int32)
    kept_rows = (positions >= resume_at[0])[:, None]
    mixed = gate_out.astype(jnp.float32) * (convolved + skip_bias[None, :] * signal)
    mixed = jnp.where(kept_rows, mixed, jnp.zeros_like(mixed)).astype(jnp.bfloat16)
    return jnp.dot(mixed, out_weight, preferred_element_type=jnp.float32).astype(jnp.bfloat16)
```

```python
import functools
import math

import jax
import jax.numpy as jnp
import numpy as np
from jax import lax
from jax.experimental import pallas as pl
from jax.experimental.pallas import tpu as pltpu
from jax.sharding import PartitionSpec as P

BF16 = jnp.bfloat16
F32 = jnp.float32
TILE = 128
LENGTH = TILE * TILE


def split_table(table):
    high = table.astype(jnp.bfloat16)
    low = (table - high.astype(np.float64)).astype(jnp.bfloat16)
    return high, low


@functools.lru_cache(None)
def tables():
    index = np.arange(TILE, dtype=np.float64)
    outer = 2 * math.pi * np.outer(4 * index + 1, index)
    turn = outer / 512
    first = np.concatenate([np.cos(turn), -np.sin(turn)], 0)
    first_high, first_low = split_table(first)
    last_high, last_low = split_table(first.T / LENGTH)
    twist = outer / (4 * LENGTH)
    angle = 2 * math.pi * np.outer(index, index) / TILE
    cosine, sine = np.cos(angle), np.sin(angle)
    second = np.block([[cosine, -sine], [sine, cosine]])
    second_high, second_low = split_table(second)
    back_high, back_low = split_table(second.T)
    return (
        np.concatenate([first_high, first_low], 1),
        np.concatenate([second_high, second_high, second_low], 0),
        np.concatenate([back_high, back_high, back_low], 0),
        np.concatenate([last_high, last_high, last_low], 1),
        np.cos(twist).astype(np.float32),
        np.sin(twist).astype(np.float32),
    )


def halves(array):
    high = array.astype(BF16)
    return high, (array - high.astype(F32)).astype(BF16)


def matmul(left, right):
    return jnp.dot(left, right, preferred_element_type=F32)


def pack_kernel(gate_in, value_in, taps, out):
    signal = gate_in[...].astype(F32) * value_in[...].astype(F32)
    out[:, 0, 0] = signal.T.astype(BF16).reshape(16, 16, TILE)
    out[:, 1, 0] = taps[...].T.astype(BF16).reshape(16, 16, TILE)


def pack(gate_in, value_in, taps):
    rows, channels = value_in.shape
    block = pl.BlockSpec((TILE, channels), lambda b: (b, 0))
    return pl.pallas_call(
        pack_kernel,
        grid=(rows // TILE,),
        in_specs=[block] * 3,
        out_specs=pl.BlockSpec((16, 2, 1, 16, TILE), lambda b: (0, 0, b, 0, 0)),
        out_shape=jax.ShapeDtypeStruct((16, 2, rows // TILE, 16, TILE), BF16),
        name="pack",
    )(gate_in, value_in, taps)


def conv_kernel(group, data, first, second, back, last, cosine, sine, out, signal, taps, total):
    shards, _, blocks, channels, _ = data.shape
    rows = blocks * channels

    @pl.loop(0, shards)
    def _(a):
        part = pl.ds(pl.multiple_of(a * rows, rows), rows)
        signal[part, :] = data[a, 0].astype(F32).reshape(rows, TILE)
        taps[part, :] = data[a, 1].astype(F32).reshape(rows, TILE)

    @pl.loop(0, channels // group)
    def _(step):
        cos, sin = cosine[...], sine[...]
        picks = [pl.ds(step * group + g, TILE, stride=channels) for g in range(group)]
        pieces = []
        for pick in picks:
            pair = jnp.concatenate([signal[pick, :], taps[pick, :]], 1).astype(BF16)
            lifted = matmul(first[...], jnp.concatenate([pair, pair], 0))
            for side in range(2):
                real = lifted[:TILE, side * TILE : (side + 1) * TILE]
                imag = lifted[TILE:, side * TILE : (side + 1) * TILE]
                turned = jnp.concatenate([real * cos + imag * sin, imag * cos - real * sin], 1)
                high, low = halves(turned)
                pieces.append(jnp.concatenate([high, low, high], 1))
        spectra = matmul(jnp.concatenate(pieces, 0), second[...])
        pieces = []
        for g in range(group):
            left = spectra[2 * g * TILE : (2 * g + 1) * TILE]
            right = spectra[(2 * g + 1) * TILE : (2 * g + 2) * TILE]
            real = left[:, :TILE] * right[:, :TILE] - left[:, TILE:] * right[:, TILE:]
            imag = left[:, :TILE] * right[:, TILE:] + left[:, TILE:] * right[:, :TILE]
            high, low = halves(jnp.concatenate([real, imag], 1))
            pieces.append(jnp.concatenate([high, low, high], 1))
        restored = matmul(jnp.concatenate(pieces, 0), back[...])
        pieces = []
        for g in range(group):
            real = restored[g * TILE : (g + 1) * TILE, :TILE]
            imag = restored[g * TILE : (g + 1) * TILE, TILE:]
            turned = jnp.concatenate([real * cos - imag * sin, imag * cos + real * sin], 0)
            high, low = halves(turned)
            pieces.append(jnp.concatenate([high, low, high], 0))
        result = matmul(last[...], jnp.concatenate(pieces, 1))
        for g, pick in enumerate(picks):
            total[pick, :] = result[:, g * TILE : (g + 1) * TILE]

    @pl.loop(0, shards)
    def _(a):
        part = pl.ds(pl.multiple_of(a * rows, rows), rows)
        out[a] = total[part, :].astype(BF16).reshape(blocks, channels, TILE)


def convolve(data, group=4):
    shards, _, blocks, channels, _ = data.shape
    whole = pltpu.VMEM((shards * blocks * channels, TILE), F32)
    space = pl.BlockSpec(memory_space=pltpu.VMEM)
    return pl.pallas_call(
        functools.partial(conv_kernel, group),
        in_specs=[space] * 7,
        out_specs=space,
        out_shape=jax.ShapeDtypeStruct((shards, blocks, channels, TILE), BF16),
        scratch_shapes=[whole] * 3,
        compiler_params=pltpu.CompilerParams(vmem_limit_bytes=48 << 20),
        name="convolve",
    )(data, *(jnp.asarray(table) for table in tables()))


def mix_kernel(start, conv, gate_out, gate_in, value_in, skip, out):
    rows = TILE
    first = pl.program_id(0) * rows + lax.axis_index("seq") * (rows * pl.num_programs(0))
    position = first + lax.broadcasted_iota(jnp.int32, (rows, 1), 0)
    signal = gate_in[...].astype(F32) * value_in[...].astype(F32)
    convolved = conv[:, 0].astype(F32).reshape(-1, TILE).T
    mixed = gate_out[...].astype(F32) * (convolved + skip[...] * signal)
    out[...] = jnp.where(position >= start[0], mixed, 0.0).astype(BF16)


def mix(resume_at, conv, gate_out, gate_in, value_in, skip_bias):
    rows, channels = value_in.shape
    block = pl.BlockSpec((TILE, channels), lambda b: (b, 0))
    return pl.pallas_call(
        mix_kernel,
        grid=(rows // TILE,),
        in_specs=[
            pl.BlockSpec(memory_space=pltpu.SMEM),
            pl.BlockSpec((16, 1, 16, TILE), lambda b: (0, b, 0, 0)),
            block,
            block,
            block,
            pl.BlockSpec((1, channels), lambda b: (0, 0)),
        ],
        out_specs=block,
        out_shape=jax.ShapeDtypeStruct((rows, channels), BF16),
        name="mix",
    )(resume_at, conv, gate_out, gate_in, value_in, skip_bias[None, :])


def project_kernel(mixed, weight, out):
    total = matmul(mixed[0], weight[0])
    for k in range(1, mixed.shape[0]):
        total = total + matmul(mixed[k], weight[k])
    out[...] = total.astype(BF16)


def project(mixed, weight, tile=256):
    parts, rows, channels = mixed.shape
    features = weight.shape[-1]
    return pl.pallas_call(
        project_kernel,
        grid=(rows // tile,),
        in_specs=[
            pl.BlockSpec((parts, tile, channels), lambda i: (0, i, 0)),
            pl.BlockSpec((parts, channels, features), lambda i: (0, 0, 0)),
        ],
        out_specs=pl.BlockSpec((tile, features), lambda i: (i, 0)),
        out_shape=jax.ShapeDtypeStruct((rows, features), BF16),
        compiler_params=pltpu.CompilerParams(vmem_limit_bytes=32 << 20),
        name="project",
    )(mixed, weight)


def on_device(gate_out, gate_in, value_in, filter_taps, skip_bias, resume_at, out_weight):
    members = lax.axis_size("chan")
    channels, features = out_weight.shape
    weight = lax.all_to_all(
        out_weight.reshape(channels, members, features // members).swapaxes(0, 1),
        "chan",
        split_axis=0,
        concat_axis=0,
        tiled=True,
    )
    packed = pack(gate_in, value_in, filter_taps)
    data = lax.all_to_all(packed, "seq", split_axis=0, concat_axis=0, tiled=True)
    conv = lax.all_to_all(convolve(data), "seq", split_axis=0, concat_axis=0, tiled=True)
    mixed = mix(resume_at, conv, gate_out, gate_in, value_in, skip_bias)
    return project(lax.all_gather(mixed, "chan", axis=0), weight)


def solution(mesh):
    placed = (
        P("seq", "chan"),
        P("seq", "chan"),
        P("seq", "chan"),
        P("seq", "chan"),
        P("chan"),
        P(),
        P("chan", None),
    )
    return jax.shard_map(
        on_device, mesh=mesh, in_specs=placed, out_specs=P("seq", "chan"), check_vma=False
    )
```

```python
import functools
import math

import jax
import jax.numpy as jnp
import numpy as np
from jax import lax
from jax.experimental import pallas as pl
from jax.experimental.pallas import tpu as pltpu
from jax.sharding import PartitionSpec as P

BF16 = jnp.bfloat16
F32 = jnp.float32
TILE = 128
LENGTH = TILE * TILE


def split_table(table):
    high = table.astype(jnp.bfloat16)
    low = (table - high.astype(np.float64)).astype(jnp.bfloat16)
    return high, low


@functools.lru_cache(None)
def tables():
    index = np.arange(TILE, dtype=np.float64)
    outer = 2 * math.pi * np.outer(4 * index + 1, index)
    turn = outer / 512
    first = np.concatenate([np.cos(turn), -np.sin(turn)], 0)
    first_high, first_low = split_table(first)
    last_high, last_low = split_table(first.T / LENGTH)
    twist = outer / (4 * LENGTH)
    angle = 2 * math.pi * np.outer(index, index) / TILE
    cosine, sine = np.cos(angle), np.sin(angle)
    second = np.block([[cosine, -sine], [sine, cosine]])
    second_high, second_low = split_table(second)
    back_high, back_low = split_table(second.T)
    turns = np.concatenate(
        [
            np.concatenate([first_high, first_low], 1),
            second_high,
            second_high,
            second_low,
            back_high,
            back_high,
            back_low,
            last_high,
            last_high,
            last_low,
        ],
        0,
    )
    twists = np.concatenate([np.cos(twist), np.sin(twist)], 0).astype(np.float32)
    return turns, twists


def halves(array):
    high = array.astype(BF16)
    return high, (array - high.astype(F32)).astype(BF16)


def matmul(left, right):
    return jnp.dot(left, right, preferred_element_type=F32)


def pack_kernel(gate_in, value_in, taps, out):
    for b in range(out.shape[2]):
        rows = slice(b * TILE, (b + 1) * TILE)
        signal = gate_in[rows].astype(F32) * value_in[rows].astype(F32)
        out[:, 0, b] = signal.astype(BF16).T.reshape(16, 16, TILE)
        out[:, 1, b] = taps[rows].astype(BF16).T.reshape(16, 16, TILE)


def pack(gate_in, value_in, taps, blocks=4):
    rows, channels = value_in.shape
    block = pl.BlockSpec((blocks * TILE, channels), lambda b: (b, 0))
    return pl.pallas_call(
        pack_kernel,
        grid=(rows // (blocks * TILE),),
        in_specs=[block] * 3,
        out_specs=pl.BlockSpec((16, 2, blocks, 16, TILE), lambda b: (0, 0, b, 0, 0)),
        out_shape=jax.ShapeDtypeStruct((16, 2, rows // TILE, 16, TILE), BF16),
        name="pack",
    )(gate_in, value_in, taps)


def conv_kernel(group, data, turns, twists, out, signal, taps, total):
    shards, _, blocks, channels, _ = data.shape
    rows = blocks * channels
    span = 2 * TILE
    first, second, back = turns.at[:span], turns.at[span : 4 * span], turns.at[4 * span : 7 * span]
    cosine, sine = twists.at[:TILE], twists.at[TILE:]
    last = [turns[7 * span + k * TILE : 7 * span + (k + 1) * TILE, :] for k in range(3)]

    @pl.loop(0, shards)
    def _(a):
        part = pl.ds(pl.multiple_of(a * rows, rows), rows)
        signal[part, :] = data[a, 0].astype(F32).reshape(rows, TILE)
        taps[part, :] = data[a, 1].astype(F32).reshape(rows, TILE)

    @pl.loop(0, channels // group)
    def _(step):
        cos, sin = cosine[...], sine[...]
        picks = [pl.ds(step * group + g, TILE, stride=channels) for g in range(group)]
        pieces = []
        for pick in picks:
            pair = jnp.concatenate([signal[pick, :], taps[pick, :]], 1).astype(BF16)
            lifted = matmul(first[...], jnp.concatenate([pair, pair], 0))
            for side in range(2):
                real = lifted[:TILE, side * TILE : (side + 1) * TILE]
                imag = lifted[TILE:, side * TILE : (side + 1) * TILE]
                turned = jnp.concatenate([real * cos + imag * sin, imag * cos - real * sin], 1)
                high, low = halves(turned)
                pieces.append(jnp.concatenate([high, low, high], 1))
        spectra = matmul(jnp.concatenate(pieces, 0), second[...])
        pieces = []
        for g in range(group):
            left = spectra[2 * g * TILE : (2 * g + 1) * TILE]
            right = spectra[(2 * g + 1) * TILE : (2 * g + 2) * TILE]
            real = left[:, :TILE] * right[:, :TILE] - left[:, TILE:] * right[:, TILE:]
            imag = left[:, :TILE] * right[:, TILE:] + left[:, TILE:] * right[:, :TILE]
            high, low = halves(jnp.concatenate([real, imag], 1))
            pieces.append(jnp.concatenate([high, low, high], 1))
        restored = matmul(jnp.concatenate(pieces, 0), back[...])
        pieces = []
        for g in range(group):
            real = restored[g * TILE : (g + 1) * TILE, :TILE]
            imag = restored[g * TILE : (g + 1) * TILE, TILE:]
            turned = jnp.concatenate([real * cos - imag * sin, imag * cos + real * sin], 0)
            high, low = halves(turned)
            pieces.append(jnp.concatenate([high, low, high], 0))
        result = matmul(jnp.concatenate(last, 1), jnp.concatenate(pieces, 1))
        for g, pick in enumerate(picks):
            total[pick, :] = result[:, g * TILE : (g + 1) * TILE]

    @pl.loop(0, shards)
    def _(a):
        part = pl.ds(pl.multiple_of(a * rows, rows), rows)
        out[a] = total[part, :].astype(BF16).reshape(blocks, channels, TILE)


def convolve(data, group=8):
    shards, _, blocks, channels, _ = data.shape
    whole = pltpu.VMEM((shards * blocks * channels, TILE), F32)
    space = pl.BlockSpec(memory_space=pltpu.VMEM)
    return pl.pallas_call(
        functools.partial(conv_kernel, group),
        in_specs=[space] * 3,
        out_specs=space,
        out_shape=jax.ShapeDtypeStruct((shards, blocks, channels, TILE), BF16),
        scratch_shapes=[whole] * 3,
        compiler_params=pltpu.CompilerParams(vmem_limit_bytes=28 << 20),
        cost_estimate=pl.CostEstimate(flops=10**10, bytes_accessed=1 << 22, transcendentals=0),
        name="convolve",
    )(data, *(jnp.asarray(table) for table in tables()))


def mix_kernel(start, conv, gate_out, gate_in, value_in, skip, _, top, low):
    rows = gate_out.shape[0]
    step = pl.program_id(0)
    shard = lax.axis_index("seq") * (rows * pl.num_programs(0))

    def fill(out):
        for b in range(rows // TILE):
            part = slice(b * TILE, (b + 1) * TILE)
            first = shard + step * rows + b * TILE
            position = first + lax.broadcasted_iota(jnp.int32, (TILE, 1), 0)
            signal = gate_in[part].astype(F32) * value_in[part].astype(F32)
            convolved = conv[:, b].reshape(-1, TILE).T.astype(F32)
            mixed = gate_out[part].astype(F32) * (convolved + skip[...] * signal)
            out[part] = jnp.where(position >= start[0], mixed, 0.0).astype(BF16)

    @pl.when(step == 0)
    def _():
        fill(top)

    @pl.when(step == 1)
    def _():
        fill(low)


def mix(resume_at, conv, gate_out, gate_in, value_in, skip_bias, after):
    rows, channels = value_in.shape
    half = rows // 2
    block = pl.BlockSpec((half, channels), lambda i: (i, 0))
    kept = pl.BlockSpec((half, channels), lambda i: (0, 0))
    return pl.pallas_call(
        mix_kernel,
        grid=(2,),
        in_specs=[
            pl.BlockSpec(memory_space=pltpu.SMEM),
            pl.BlockSpec((16, half // TILE, 16, TILE), lambda i: (0, i, 0, 0)),
            block,
            block,
            block,
            pl.BlockSpec((1, channels), lambda i: (0, 0)),
            pl.BlockSpec(memory_space=pl.ANY),
        ],
        out_specs=[kept] * 2,
        out_shape=[jax.ShapeDtypeStruct((half, channels), BF16)] * 2,
        compiler_params=pltpu.CompilerParams(vmem_limit_bytes=12 << 20),
        name="mix",
    )(resume_at, conv, gate_out, gate_in, value_in, skip_bias[None, :], after)


def toward(array, step, swap):
    pairs = [(z * 2 + c, (z + step) % 4 * 2 + (c ^ swap)) for z in range(4) for c in range(2)]
    return lax.ppermute(array, "chan", pairs)


ROUTES = tuple((step, swap) for step in range(4) for swap in range(2))


def split_kernel(weight, _, *outs):
    me = lax.axis_index("chan")
    features = outs[0].shape[1]
    core = lax.rem(me, 2)
    for out, (step, swap) in zip(outs, ROUTES):
        target = lax.rem(me // 2 + step, 4) * 2 + (1 - core if swap else core)
        out[...] = weight[:, pl.ds(pl.multiple_of(target * features, features), features)]


def split_weight(weight, after, tile=128):
    channels, features = weight.shape
    members = len(ROUTES)
    width = features // members
    return pl.pallas_call(
        split_kernel,
        grid=(channels // tile,),
        in_specs=[
            pl.BlockSpec((tile, features), lambda i: (i, 0)),
            pl.BlockSpec(memory_space=pl.ANY),
        ],
        out_specs=[pl.BlockSpec((tile, width), lambda i: (i, 0))] * members,
        out_shape=[jax.ShapeDtypeStruct((channels, width), BF16)] * members,
        name="split_weight",
    )(weight, after)


def mark_kernel(*refs):
    refs[-1][...] = jnp.zeros_like(refs[-1])


def mark(arrays):
    return pl.pallas_call(
        mark_kernel,
        in_specs=[pl.BlockSpec(memory_space=pl.ANY)] * len(arrays),
        out_shape=jax.ShapeDtypeStruct((8, TILE), F32),
        cost_estimate=pl.CostEstimate(flops=10**10, bytes_accessed=0, transcendentals=0),
        name="mark",
    )(*arrays)


def tie_kernel(count, *refs):
    for source, target in zip(refs[:count], refs[-count:]):
        target[...] = source[...]


def tie(arrays, after):
    space = pl.BlockSpec(memory_space=pltpu.VMEM)
    count = len(arrays)
    return pl.pallas_call(
        functools.partial(tie_kernel, count),
        in_specs=[space] * count + [pl.BlockSpec(memory_space=pl.ANY)] * len(after),
        out_specs=[space] * count,
        out_shape=[jax.ShapeDtypeStruct(array.shape, array.dtype) for array in arrays],
        input_output_aliases={k: k for k in range(count)},
        compiler_params=pltpu.CompilerParams(vmem_limit_bytes=12 << 20),
        name="tie",
    )(*arrays, *after)


def project_kernel(*refs):
    mixed, weight, out = refs[:16], refs[16:24], refs[24]

    def fill(pieces):
        total = matmul(pieces[0][...], weight[0][...])
        for piece, part in zip(pieces[1:], weight[1:]):
            total = total + matmul(piece[...], part[...])
        out[...] = total.astype(BF16)

    for half in range(2):
        pl.when(pl.program_id(0) == half)(
            functools.partial(fill, mixed[8 * half : 8 * half + 8])
        )


def project(top, low, weight):
    rows = top[0].shape[0]
    features = weight[0].shape[1]
    return pl.pallas_call(
        project_kernel,
        grid=(2,),
        in_specs=[pl.BlockSpec(memory_space=pltpu.VMEM)] * 24,
        out_specs=pl.BlockSpec((rows, features), lambda i: (i, 0)),
        out_shape=jax.ShapeDtypeStruct((2 * rows, features), BF16),
        compiler_params=pltpu.CompilerParams(vmem_limit_bytes=16 << 20),
        name="project",
    )(*top, *low, *weight)


def on_device(gate_out, gate_in, value_in, filter_taps, skip_bias, resume_at, out_weight):
    packed = pack(gate_in, value_in, filter_taps)
    data = lax.all_to_all(packed, "seq", split_axis=0, concat_axis=0, tiled=True)
    weight = split_weight(out_weight, packed)
    weight = [toward(w, *route) if any(route) else w for w, route in zip(weight, ROUTES)]
    conv = lax.all_to_all(convolve(data), "seq", split_axis=0, concat_axis=0, tiled=True)
    top, low = mix(resume_at, conv, gate_out, gate_in, value_in, skip_bias, mark(weight))
    up_top, down_low = toward(top, 1, 0), toward(low, 3, 0)
    up_low, down_top = toward(low, 1, 0), toward(top, 3, 0)
    far_top, far_low = toward(up_top, 1, 0), toward(down_low, 3, 0)
    up_top_other, down_low_other = toward(up_top, 0, 1), toward(down_low, 0, 1)
    up_low, down_top = tie([up_low, down_top], [up_top_other, down_low_other])
    tops = [top, toward(top, 0, 1), up_top, up_top_other, far_top, toward(far_top, 0, 1)]
    tops += [down_top, toward(down_top, 0, 1)]
    lows = [low, toward(low, 0, 1), up_low, toward(up_low, 0, 1), far_low, toward(far_low, 0, 1)]
    lows += [down_low, down_low_other]
    return project(tops, lows, weight)


def solution(mesh):
    placed = (
        P("seq", "chan"),
        P("seq", "chan"),
        P("seq", "chan"),
        P("seq", "chan"),
        P("chan"),
        P(),
        P("chan", None),
    )
    return jax.shard_map(
        on_device, mesh=mesh, in_specs=placed, out_specs=P("seq", "chan"), check_vma=False
    )
```

```python
import functools
import math

import jax
import jax.numpy as jnp
import numpy as np
from jax import lax
from jax.experimental import pallas as pl
from jax.experimental.pallas import tpu as pltpu
from jax.sharding import PartitionSpec as P

BF16 = jnp.bfloat16
F32 = jnp.float32
TILE = 128
LENGTH = TILE * TILE


def split_table(table):
    high = table.astype(jnp.bfloat16)
    low = (table - high.astype(np.float64)).astype(jnp.bfloat16)
    return high, low


@functools.lru_cache(None)
def tables():
    index = np.arange(TILE, dtype=np.float64)
    outer = 2 * math.pi * np.outer(4 * index + 1, index)
    turn = outer / 512
    first = np.concatenate([np.cos(turn), -np.sin(turn)], 0)
    first_high, first_low = split_table(first)
    last_high, last_low = split_table(first.T / LENGTH)
    twist = outer / (4 * LENGTH)
    angle = 2 * math.pi * np.outer(index, index) / TILE
    cosine, sine = np.cos(angle), np.sin(angle)
    second = np.block([[cosine, -sine], [sine, cosine]])
    second_high, second_low = split_table(second)
    back_high, back_low = split_table(second.T)
    turns = np.concatenate(
        [
            np.concatenate([first_high, first_low], 1),
            second_high,
            second_high,
            second_low,
            back_high,
            back_high,
            back_low,
            last_high,
            last_high,
            last_low,
        ],
        0,
    )
    twists = np.concatenate([np.cos(twist), np.sin(twist)], 0).astype(np.float32)
    return turns, twists


def halves(array):
    high = array.astype(BF16)
    return high, (array - high.astype(F32)).astype(BF16)


def matmul(left, right):
    return jnp.dot(left, right, preferred_element_type=F32)


def pack_kernel(gate_in, value_in, taps, out):
    for b in range(out.shape[2]):
        rows = slice(b * TILE, (b + 1) * TILE)
        signal = gate_in[rows].astype(F32) * value_in[rows].astype(F32)
        out[:, 0, b] = signal.astype(BF16).T.reshape(16, 16, TILE)
        out[:, 1, b] = taps[rows].astype(BF16).T.reshape(16, 16, TILE)


def pack(gate_in, value_in, taps, blocks=4):
    rows, channels = value_in.shape
    block = pl.BlockSpec((blocks * TILE, channels), lambda b: (b, 0))
    return pl.pallas_call(
        pack_kernel,
        grid=(rows // (blocks * TILE),),
        in_specs=[block] * 3,
        out_specs=pl.BlockSpec((16, 2, blocks, 16, TILE), lambda b: (0, 0, b, 0, 0)),
        out_shape=jax.ShapeDtypeStruct((16, 2, rows // TILE, 16, TILE), BF16),
        name="pack",
    )(gate_in, value_in, taps)


def conv_kernel(group, data, turns, twists, out, signal, taps, total):
    shards, _, blocks, channels, _ = data.shape
    rows = blocks * channels
    span = 2 * TILE
    first, second, back = turns.at[:span], turns.at[span : 4 * span], turns.at[4 * span : 7 * span]
    cosine, sine = twists.at[:TILE], twists.at[TILE:]
    last = [turns[7 * span + k * TILE : 7 * span + (k + 1) * TILE, :] for k in range(3)]

    @pl.loop(0, shards)
    def _(a):
        part = pl.ds(pl.multiple_of(a * rows, rows), rows)
        signal[part, :] = data[a, 0].astype(F32).reshape(rows, TILE)
        taps[part, :] = data[a, 1].astype(F32).reshape(rows, TILE)

    @pl.loop(0, channels // group)
    def _(step):
        cos, sin = cosine[...], sine[...]
        picks = [pl.ds(step * group + g, TILE, stride=channels) for g in range(group)]
        pieces = []
        for pick in picks:
            pair = jnp.concatenate([signal[pick, :], taps[pick, :]], 1).astype(BF16)
            lifted = matmul(first[...], jnp.concatenate([pair, pair], 0))
            for side in range(2):
                real = lifted[:TILE, side * TILE : (side + 1) * TILE]
                imag = lifted[TILE:, side * TILE : (side + 1) * TILE]
                turned = jnp.concatenate([real * cos + imag * sin, imag * cos - real * sin], 1)
                high, low = halves(turned)
                pieces.append(jnp.concatenate([high, low, high], 1))
        spectra = matmul(jnp.concatenate(pieces, 0), second[...])
        pieces = []
        for g in range(group):
            left = spectra[2 * g * TILE : (2 * g + 1) * TILE]
            right = spectra[(2 * g + 1) * TILE : (2 * g + 2) * TILE]
            real = left[:, :TILE] * right[:, :TILE] - left[:, TILE:] * right[:, TILE:]
            imag = left[:, :TILE] * right[:, TILE:] + left[:, TILE:] * right[:, :TILE]
            high, low = halves(jnp.concatenate([real, imag], 1))
            pieces.append(jnp.concatenate([high, low, high], 1))
        restored = matmul(jnp.concatenate(pieces, 0), back[...])
        pieces = []
        for g in range(group):
            real = restored[g * TILE : (g + 1) * TILE, :TILE]
            imag = restored[g * TILE : (g + 1) * TILE, TILE:]
            turned = jnp.concatenate([real * cos - imag * sin, imag * cos + real * sin], 0)
            high, low = halves(turned)
            pieces.append(jnp.concatenate([high, low, high], 0))
        result = matmul(jnp.concatenate(last, 1), jnp.concatenate(pieces, 1))
        for g, pick in enumerate(picks):
            total[pick, :] = result[:, g * TILE : (g + 1) * TILE]

    @pl.loop(0, shards)
    def _(a):
        part = pl.ds(pl.multiple_of(a * rows, rows), rows)
        out[a] = total[part, :].astype(BF16).reshape(blocks, channels, TILE)


def convolve(data, group=8):
    shards, _, blocks, channels, _ = data.shape
    whole = pltpu.VMEM((shards * blocks * channels, TILE), F32)
    space = pl.BlockSpec(memory_space=pltpu.VMEM)
    return pl.pallas_call(
        functools.partial(conv_kernel, group),
        in_specs=[space] * 3,
        out_specs=space,
        out_shape=jax.ShapeDtypeStruct((shards, blocks, channels, TILE), BF16),
        scratch_shapes=[whole] * 3,
        compiler_params=pltpu.CompilerParams(vmem_limit_bytes=28 << 20),
        cost_estimate=pl.CostEstimate(flops=10**10, bytes_accessed=1 << 22, transcendentals=0),
        name="convolve",
    )(data, *(jnp.asarray(table) for table in tables()))


def mix_kernel(start, conv, gate_out, gate_in, value_in, skip, _, top, low):
    rows = gate_out.shape[0]
    step = pl.program_id(0)
    shard = lax.axis_index("seq") * (rows * pl.num_programs(0))

    def fill(out):
        for b in range(rows // TILE):
            part = slice(b * TILE, (b + 1) * TILE)
            first = shard + step * rows + b * TILE
            position = first + lax.broadcasted_iota(jnp.int32, (TILE, 1), 0)
            signal = gate_in[part].astype(F32) * value_in[part].astype(F32)
            convolved = conv[:, b].reshape(-1, TILE).T.astype(F32)
            mixed = gate_out[part].astype(F32) * (convolved + skip[...] * signal)
            out[part] = jnp.where(position >= start[0], mixed, 0.0).astype(BF16)

    @pl.when(step == 0)
    def _():
        fill(top)

    @pl.when(step == 1)
    def _():
        fill(low)


def mix(resume_at, conv, gate_out, gate_in, value_in, skip_bias, after):
    rows, channels = value_in.shape
    half = rows // 2
    block = pl.BlockSpec((half, channels), lambda i: (i, 0))
    kept = pl.BlockSpec((half, channels), lambda i: (0, 0))
    return pl.pallas_call(
        mix_kernel,
        grid=(2,),
        in_specs=[
            pl.BlockSpec(memory_space=pltpu.SMEM),
            pl.BlockSpec((16, half // TILE, 16, TILE), lambda i: (0, i, 0, 0)),
            block,
            block,
            block,
            pl.BlockSpec((1, channels), lambda i: (0, 0)),
            pl.BlockSpec(memory_space=pl.ANY),
        ],
        out_specs=[kept] * 2,
        out_shape=[jax.ShapeDtypeStruct((half, channels), BF16)] * 2,
        compiler_params=pltpu.CompilerParams(vmem_limit_bytes=12 << 20),
        name="mix",
    )(resume_at, conv, gate_out, gate_in, value_in, skip_bias[None, :], after)


def toward(array, step, swap):
    pairs = [(z * 2 + c, (z + step) % 4 * 2 + (c ^ swap)) for z in range(4) for c in range(2)]
    return lax.ppermute(array, "chan", pairs)


ROUTES = ((1, 0), (3, 0), (1, 1), (3, 1), (2, 0), (2, 1), (0, 1), (0, 0))


def split_kernel(weight, _, *outs):
    me = lax.axis_index("chan")
    features = outs[0].shape[1]
    core = lax.rem(me, 2)
    for out, (step, swap) in zip(outs, ROUTES):
        target = lax.rem(me // 2 + step, 4) * 2 + (1 - core if swap else core)
        out[...] = weight[:, pl.ds(pl.multiple_of(target * features, features), features)]


def split_weight(weight, after, tile=128):
    channels, features = weight.shape
    members = len(ROUTES)
    width = features // members
    return pl.pallas_call(
        split_kernel,
        grid=(channels // tile,),
        in_specs=[
            pl.BlockSpec((tile, features), lambda i: (i, 0)),
            pl.BlockSpec(memory_space=pl.ANY),
        ],
        out_specs=[pl.BlockSpec((tile, width), lambda i: (i, 0))] * members,
        out_shape=[jax.ShapeDtypeStruct((channels, width), BF16)] * members,
        compiler_params=pltpu.CompilerParams(vmem_limit_bytes=12 << 20),
        name="split_weight",
    )(weight, after)


def mark_kernel(*refs):
    refs[-1][...] = jnp.zeros_like(refs[-1])


def mark(arrays):
    return pl.pallas_call(
        mark_kernel,
        in_specs=[pl.BlockSpec(memory_space=pl.ANY)] * len(arrays),
        out_shape=jax.ShapeDtypeStruct((8, TILE), F32),
        compiler_params=pltpu.CompilerParams(vmem_limit_bytes=2 << 20),
        cost_estimate=pl.CostEstimate(flops=10**10, bytes_accessed=0, transcendentals=0),
        name="mark",
    )(*arrays)


def tie_kernel(count, *refs):
    for source, target in zip(refs[:count], refs[-count:]):
        target[...] = source[...]


def tie(arrays, after):
    space = pl.BlockSpec(memory_space=pltpu.VMEM)
    count = len(arrays)
    return pl.pallas_call(
        functools.partial(tie_kernel, count),
        in_specs=[space] * count + [pl.BlockSpec(memory_space=pl.ANY)] * len(after),
        out_specs=[space] * count,
        out_shape=[jax.ShapeDtypeStruct(array.shape, array.dtype) for array in arrays],
        input_output_aliases={k: k for k in range(count)},
        compiler_params=pltpu.CompilerParams(vmem_limit_bytes=12 << 20),
        name="tie",
    )(*arrays, *after)


def project_kernel(*refs):
    mixed, weight, out = refs[:16], refs[16:24], refs[24]

    def fill(pieces):
        total = matmul(pieces[0][...], weight[0][...])
        for piece, part in zip(pieces[1:], weight[1:]):
            total = total + matmul(piece[...], part[...])
        out[...] = total.astype(BF16)

    for half in range(2):
        pl.when(pl.program_id(0) == half)(
            functools.partial(fill, mixed[8 * half : 8 * half + 8])
        )


def project(top, low, weight):
    rows = top[0].shape[0]
    features = weight[0].shape[1]
    return pl.pallas_call(
        project_kernel,
        grid=(2,),
        in_specs=[pl.BlockSpec(memory_space=pltpu.VMEM)] * 24,
        out_specs=pl.BlockSpec((rows, features), lambda i: (i, 0)),
        out_shape=jax.ShapeDtypeStruct((2 * rows, features), BF16),
        compiler_params=pltpu.CompilerParams(vmem_limit_bytes=16 << 20),
        name="project",
    )(*top, *low, *weight)


def on_device(gate_out, gate_in, value_in, filter_taps, skip_bias, resume_at, out_weight):
    packed = pack(gate_in, value_in, filter_taps)
    data = lax.all_to_all(packed, "seq", split_axis=0, concat_axis=0, tiled=True)
    weight = split_weight(out_weight, packed)
    weight = [toward(w, *route) if any(route) else w for w, route in zip(weight, ROUTES)]
    conv = lax.all_to_all(convolve(data), "seq", split_axis=0, concat_axis=0, tiled=True)
    top, low = mix(resume_at, conv, gate_out, gate_in, value_in, skip_bias, mark(weight))
    up_top, down_low = toward(top, 1, 0), toward(low, 3, 0)
    up_low, down_top = toward(low, 1, 0), toward(top, 3, 0)
    far_top, far_low = toward(up_top, 1, 0), toward(down_low, 3, 0)
    up_top_other, down_low_other = toward(up_top, 0, 1), toward(down_low, 0, 1)
    up_low, down_top = tie([up_low, down_top], [up_top_other, down_low_other])
    tops = [top, toward(top, 0, 1), up_top, up_top_other, far_top, toward(far_top, 0, 1)]
    tops += [down_top, toward(down_top, 0, 1)]
    lows = [low, toward(low, 0, 1), up_low, toward(up_low, 0, 1), far_low, toward(far_low, 0, 1)]
    lows += [down_low, down_low_other]
    weight = [weight[ROUTES.index((step, swap))] for step in range(4) for swap in range(2)]
    return project(tops, lows, weight)


def solution(mesh):
    placed = (
        P("seq", "chan"),
        P("seq", "chan"),
        P("seq", "chan"),
        P("seq", "chan"),
        P("chan"),
        P(),
        P("chan", None),
    )
    return jax.shard_map(
        on_device, mesh=mesh, in_specs=placed, out_specs=P("seq", "chan"), check_vma=False
    )
```

```python
import functools
import math

import jax
import jax.numpy as jnp
import numpy as np
from jax import lax
from jax.experimental import pallas as pl
from jax.experimental.pallas import tpu as pltpu
from jax.sharding import PartitionSpec as P

BF16 = jnp.bfloat16
F32 = jnp.float32
TILE = 128
LENGTH = TILE * TILE


def split_table(table):
    high = table.astype(jnp.bfloat16)
    low = (table - high.astype(np.float64)).astype(jnp.bfloat16)
    return high, low


@functools.lru_cache(None)
def tables():
    index = np.arange(TILE, dtype=np.float64)
    outer = 2 * math.pi * np.outer(4 * index + 1, index)
    turn = outer / 512
    first = np.concatenate([np.cos(turn), -np.sin(turn)], 0)
    first_high, first_low = split_table(first)
    last_high, last_low = split_table(first.T / LENGTH)
    twist = outer / (4 * LENGTH)
    angle = 2 * math.pi * np.outer(index, index) / TILE
    cosine, sine = np.cos(angle), np.sin(angle)
    second = np.block([[cosine, -sine], [sine, cosine]])
    second_high, second_low = split_table(second)
    back_high, back_low = split_table(second.T)
    turns = np.concatenate(
        [
            np.concatenate([first_high, first_low], 1),
            second_high,
            second_high,
            second_low,
            back_high,
            back_high,
            back_low,
            last_high,
            last_high,
            last_low,
        ],
        0,
    )
    twists = np.concatenate([np.cos(twist), np.sin(twist)], 0).astype(np.float32)
    return turns, twists


def halves(array):
    high = array.astype(BF16)
    return high, (array - high.astype(F32)).astype(BF16)


def matmul(left, right):
    return jnp.dot(left, right, preferred_element_type=F32)


def pack_kernel(gate_in, value_in, taps, out, token):
    token[...] = jnp.zeros_like(token)
    for b in range(out.shape[2]):
        rows = slice(b * TILE, (b + 1) * TILE)
        signal = gate_in[rows].astype(F32) * value_in[rows].astype(F32)
        out[:, 0, b] = signal.astype(BF16).T.reshape(16, 16, TILE)
        out[:, 1, b] = taps[rows].astype(BF16).T.reshape(16, 16, TILE)


def pack(gate_in, value_in, taps, blocks=4):
    rows, channels = value_in.shape
    block = pl.BlockSpec((blocks * TILE, channels), lambda b: (b, 0))
    return pl.pallas_call(
        pack_kernel,
        grid=(rows // (blocks * TILE),),
        in_specs=[block] * 3,
        out_specs=[
            pl.BlockSpec((16, 2, blocks, 16, TILE), lambda b: (0, 0, b, 0, 0)),
            pl.BlockSpec((8, TILE), lambda b: (0, 0)),
        ],
        out_shape=[
            jax.ShapeDtypeStruct((16, 2, rows // TILE, 16, TILE), BF16),
            jax.ShapeDtypeStruct((8, TILE), F32),
        ],
        name="pack",
    )(gate_in, value_in, taps)


def conv_kernel(group, data, turns, twists, out, signal, taps, total):
    shards, _, blocks, channels, _ = data.shape
    rows = blocks * channels
    span = 2 * TILE
    first, second, back = turns.at[:span], turns.at[span : 4 * span], turns.at[4 * span : 7 * span]
    cosine, sine = twists.at[:TILE], twists.at[TILE:]
    last = [turns[7 * span + k * TILE : 7 * span + (k + 1) * TILE, :] for k in range(3)]

    @pl.loop(0, shards)
    def _(a):
        part = pl.ds(pl.multiple_of(a * rows, rows), rows)
        signal[part, :] = data[a, 0].astype(F32).reshape(rows, TILE)
        taps[part, :] = data[a, 1].astype(F32).reshape(rows, TILE)

    @pl.loop(0, channels // group)
    def _(step):
        cos, sin = cosine[...], sine[...]
        picks = [pl.ds(step * group + g, TILE, stride=channels) for g in range(group)]
        pieces = []
        for pick in picks:
            pair = jnp.concatenate([signal[pick, :], taps[pick, :]], 1).astype(BF16)
            lifted = matmul(first[...], jnp.concatenate([pair, pair], 0))
            for side in range(2):
                real = lifted[:TILE, side * TILE : (side + 1) * TILE]
                imag = lifted[TILE:, side * TILE : (side + 1) * TILE]
                turned = jnp.concatenate([real * cos + imag * sin, imag * cos - real * sin], 1)
                high, low = halves(turned)
                pieces.append(jnp.concatenate([high, low, high], 1))
        spectra = matmul(jnp.concatenate(pieces, 0), second[...])
        pieces = []
        for g in range(group):
            left = spectra[2 * g * TILE : (2 * g + 1) * TILE]
            right = spectra[(2 * g + 1) * TILE : (2 * g + 2) * TILE]
            real = left[:, :TILE] * right[:, :TILE] - left[:, TILE:] * right[:, TILE:]
            imag = left[:, :TILE] * right[:, TILE:] + left[:, TILE:] * right[:, :TILE]
            high, low = halves(jnp.concatenate([real, imag], 1))
            pieces.append(jnp.concatenate([high, low, high], 1))
        restored = matmul(jnp.concatenate(pieces, 0), back[...])
        pieces = []
        for g in range(group):
            real = restored[g * TILE : (g + 1) * TILE, :TILE]
            imag = restored[g * TILE : (g + 1) * TILE, TILE:]
            turned = jnp.concatenate([real * cos - imag * sin, imag * cos + real * sin], 0)
            high, low = halves(turned)
            pieces.append(jnp.concatenate([high, low, high], 0))
        result = matmul(jnp.concatenate(last, 1), jnp.concatenate(pieces, 1))
        for g, pick in enumerate(picks):
            total[pick, :] = result[:, g * TILE : (g + 1) * TILE]

    @pl.loop(0, shards)
    def _(a):
        part = pl.ds(pl.multiple_of(a * rows, rows), rows)
        out[a] = total[part, :].astype(BF16).reshape(blocks, channels, TILE)


def convolve(data, group=8):
    shards, _, blocks, channels, _ = data.shape
    whole = pltpu.VMEM((shards * blocks * channels, TILE), F32)
    space = pl.BlockSpec(memory_space=pltpu.VMEM)
    return pl.pallas_call(
        functools.partial(conv_kernel, group),
        in_specs=[space] * 3,
        out_specs=space,
        out_shape=jax.ShapeDtypeStruct((shards, blocks, channels, TILE), BF16),
        scratch_shapes=[whole] * 3,
        compiler_params=pltpu.CompilerParams(vmem_limit_bytes=28 << 20),
        cost_estimate=pl.CostEstimate(flops=10**10, bytes_accessed=1 << 22, transcendentals=0),
        name="convolve",
    )(data, *(jnp.asarray(table) for table in tables()))


def mix_kernel(start, conv, gate_out, gate_in, value_in, skip, _, top, low):
    rows = gate_out.shape[0]
    step = pl.program_id(0)
    shard = lax.axis_index("seq") * (rows * pl.num_programs(0))

    def fill(out):
        for b in range(rows // TILE):
            part = slice(b * TILE, (b + 1) * TILE)
            first = shard + step * rows + b * TILE
            position = first + lax.broadcasted_iota(jnp.int32, (TILE, 1), 0)
            signal = gate_in[part].astype(F32) * value_in[part].astype(F32)
            convolved = conv[:, b].reshape(-1, TILE).T.astype(F32)
            mixed = gate_out[part].astype(F32) * (convolved + skip[...] * signal)
            out[part] = jnp.where(position >= start[0], mixed, 0.0).astype(BF16)

    @pl.when(step == 0)
    def _():
        fill(top)

    @pl.when(step == 1)
    def _():
        fill(low)


def mix(resume_at, conv, gate_out, gate_in, value_in, skip_bias, after):
    rows, channels = value_in.shape
    half = rows // 2
    block = pl.BlockSpec((half, channels), lambda i: (i, 0))
    kept = pl.BlockSpec((half, channels), lambda i: (0, 0))
    return pl.pallas_call(
        mix_kernel,
        grid=(2,),
        in_specs=[
            pl.BlockSpec(memory_space=pltpu.SMEM),
            pl.BlockSpec((16, half // TILE, 16, TILE), lambda i: (0, i, 0, 0)),
            block,
            block,
            block,
            pl.BlockSpec((1, channels), lambda i: (0, 0)),
            pl.BlockSpec(memory_space=pl.ANY),
        ],
        out_specs=[kept] * 2,
        out_shape=[jax.ShapeDtypeStruct((half, channels), BF16)] * 2,
        compiler_params=pltpu.CompilerParams(vmem_limit_bytes=12 << 20),
        name="mix",
    )(resume_at, conv, gate_out, gate_in, value_in, skip_bias[None, :], after)


def toward(array, step, swap):
    pairs = [(z * 2 + c, (z + step) % 4 * 2 + (c ^ swap)) for z in range(4) for c in range(2)]
    return lax.ppermute(array, "chan", pairs)


ROUTES = ((1, 0), (3, 0), (1, 1), (3, 1), (2, 0), (2, 1), (0, 1), (0, 0))


def split_kernel(weight, _, *outs):
    me = lax.axis_index("chan")
    features = outs[0].shape[1]
    core = lax.rem(me, 2)
    for out, (step, swap) in zip(outs, ROUTES):
        target = lax.rem(me // 2 + step, 4) * 2 + (1 - core if swap else core)
        out[...] = weight[:, pl.ds(pl.multiple_of(target * features, features), features)]


def split_weight(weight, after, tile=128):
    channels, features = weight.shape
    members = len(ROUTES)
    width = features // members
    return pl.pallas_call(
        split_kernel,
        grid=(channels // tile,),
        in_specs=[
            pl.BlockSpec((tile, features), lambda i: (i, 0)),
            pl.BlockSpec(memory_space=pl.ANY),
        ],
        out_specs=[pl.BlockSpec((tile, width), lambda i: (i, 0))] * members,
        out_shape=[jax.ShapeDtypeStruct((channels, width), BF16)] * members,
        compiler_params=pltpu.CompilerParams(vmem_limit_bytes=12 << 20),
        name="split_weight",
    )(weight, after)


def mark_kernel(*refs):
    refs[-1][...] = jnp.zeros_like(refs[-1])


def mark(arrays):
    return pl.pallas_call(
        mark_kernel,
        in_specs=[pl.BlockSpec(memory_space=pl.ANY)] * len(arrays),
        out_shape=jax.ShapeDtypeStruct((8, TILE), F32),
        compiler_params=pltpu.CompilerParams(vmem_limit_bytes=2 << 20),
        cost_estimate=pl.CostEstimate(flops=10**10, bytes_accessed=0, transcendentals=0),
        name="mark",
    )(*arrays)


def fold_kernel(*refs):
    top, low, weight = refs[:4], refs[4:8], refs[8:13]
    partial, first, second = refs[13:]
    rows = top[0].shape[0]
    for half, pieces in enumerate((top, low)):
        total = None
        for piece, k in zip(pieces, ((0, 1, 2, 3), (0, 3, 4, 1))[half]):
            term = matmul(piece[...], weight[k][...])
            total = term if total is None else total + term
        partial[half * rows : half * rows + rows] = total
    first[...] = top[3][...]
    second[...] = low[3][...]


def fold(top, low, weight):
    rows = top[0].shape[0]
    features = weight[0].shape[1]
    space = pl.BlockSpec(memory_space=pltpu.VMEM)
    piece = jax.ShapeDtypeStruct(top[0].shape, BF16)
    return pl.pallas_call(
        fold_kernel,
        in_specs=[space] * 13,
        out_specs=[space] * 3,
        out_shape=[jax.ShapeDtypeStruct((2 * rows, features), F32), piece, piece],
        compiler_params=pltpu.CompilerParams(vmem_limit_bytes=12 << 20),
        name="fold",
    )(*top, *low, *weight)


def project_kernel(*refs):
    mixed, weight, partial, out = refs[:8], refs[8:13], refs[13], refs[14]
    rows = out.shape[0]

    def fill(half):
        total = partial[half * rows : half * rows + rows]
        places = ((0, 1, 2, 3), (0, 1, 2, 4))[half]
        for piece, k in zip(mixed[4 * half : 4 * half + 4], places):
            total = total + matmul(piece[...], weight[k][...])
        out[...] = total.astype(BF16)

    for half in range(2):
        pl.when(pl.program_id(0) == half)(functools.partial(fill, half))


def project(top, low, weight, partial):
    rows = top[0].shape[0]
    features = weight[0].shape[1]
    return pl.pallas_call(
        project_kernel,
        grid=(2,),
        in_specs=[pl.BlockSpec(memory_space=pltpu.VMEM)] * 14,
        out_specs=pl.BlockSpec((rows, features), lambda i: (i, 0)),
        out_shape=jax.ShapeDtypeStruct((2 * rows, features), BF16),
        compiler_params=pltpu.CompilerParams(vmem_limit_bytes=12 << 20),
        name="project",
    )(*top, *low, *weight, partial)


def on_device(gate_out, gate_in, value_in, filter_taps, skip_bias, resume_at, out_weight):
    packed, token = pack(gate_in, value_in, filter_taps)
    data = lax.all_to_all(packed, "seq", split_axis=0, concat_axis=0, tiled=True)
    weight = split_weight(out_weight, token)
    weight = [toward(w, *route) if any(route) else w for w, route in zip(weight, ROUTES)]
    conv = lax.all_to_all(convolve(data), "seq", split_axis=0, concat_axis=0, tiled=True)
    top, low = mix(resume_at, conv, gate_out, gate_in, value_in, skip_bias, mark(weight))
    up_top, down_low = toward(top, 1, 0), toward(low, 3, 0)
    up_low, down_top = toward(low, 1, 0), toward(top, 3, 0)
    far_top, far_low = toward(up_top, 1, 0), toward(down_low, 3, 0)
    up_top_other, down_low_other = toward(up_top, 0, 1), toward(down_low, 0, 1)
    weight = {route: weight[ROUTES.index(route)] for route in ROUTES}
    factors = [weight[route] for route in ((0, 0), (1, 0), (1, 1), (3, 0), (3, 1))]
    partial, down_top, up_low = fold(
        [top, up_top, up_top_other, down_top], [low, down_low, down_low_other, up_low], factors
    )
    tops = [toward(top, 0, 1), far_top, toward(far_top, 0, 1), toward(down_top, 0, 1)]
    lows = [toward(low, 0, 1), far_low, toward(far_low, 0, 1), toward(up_low, 0, 1)]
    factors = [weight[route] for route in ((0, 1), (2, 0), (2, 1), (3, 1), (1, 1))]
    return project(tops, lows, factors, partial)


def solution(mesh):
    placed = (
        P("seq", "chan"),
        P("seq", "chan"),
        P("seq", "chan"),
        P("seq", "chan"),
        P("chan"),
        P(),
        P("chan", None),
    )
    return jax.shard_map(
        on_device, mesh=mesh, in_specs=placed, out_specs=P("seq", "chan"), check_vma=False
    )
```

```python
import functools
import math

import jax
import jax.numpy as jnp
import numpy as np
from jax import lax
from jax.experimental import pallas as pl
from jax.experimental.pallas import tpu as pltpu
from jax.sharding import PartitionSpec as P

BF16 = jnp.bfloat16
F32 = jnp.float32
TILE = 128
LENGTH = TILE * TILE


def split_table(table):
    high = table.astype(jnp.bfloat16)
    low = (table - high.astype(np.float64)).astype(jnp.bfloat16)
    return high, low


@functools.lru_cache(None)
def tables():
    index = np.arange(TILE, dtype=np.float64)
    outer = 2 * math.pi * np.outer(4 * index + 1, index)
    turn = outer / 512
    first = np.concatenate([np.cos(turn), -np.sin(turn)], 0)
    first_high, first_low = split_table(first)
    last_high, last_low = split_table(first.T / LENGTH)
    twist = outer / (4 * LENGTH)
    angle = 2 * math.pi * np.outer(index, index) / TILE
    cosine, sine = np.cos(angle), np.sin(angle)
    second = np.block([[cosine, -sine], [sine, cosine]])
    second_high, second_low = split_table(second)
    back_high, back_low = split_table(second.T)
    turns = np.concatenate(
        [
            np.concatenate([first_high, first_low], 1),
            second_high,
            second_high,
            second_low,
            back_high,
            back_high,
            back_low,
            last_high,
            last_high,
            last_low,
        ],
        0,
    )
    twists = np.concatenate([np.cos(twist), np.sin(twist)], 0).astype(np.float32)
    return turns, twists


def halves(array):
    high = array.astype(BF16)
    return high, (array - high.astype(F32)).astype(BF16)


def matmul(left, right):
    return jnp.dot(left, right, preferred_element_type=F32)


def pack_kernel(gate_in, value_in, taps, out, token):
    token[...] = jnp.zeros_like(token)
    for b in range(out.shape[2]):
        rows = slice(b * TILE, (b + 1) * TILE)
        signal = gate_in[rows].astype(F32) * value_in[rows].astype(F32)
        out[:, 0, b] = signal.astype(BF16).T.reshape(16, 16, TILE)
        out[:, 1, b] = taps[rows].astype(BF16).T.reshape(16, 16, TILE)


def pack(gate_in, value_in, taps, blocks=4):
    rows, channels = value_in.shape
    block = pl.BlockSpec((blocks * TILE, channels), lambda b: (b, 0))
    return pl.pallas_call(
        pack_kernel,
        grid=(rows // (blocks * TILE),),
        in_specs=[block] * 3,
        out_specs=[
            pl.BlockSpec((16, 2, blocks, 16, TILE), lambda b: (0, 0, b, 0, 0)),
            pl.BlockSpec((8, TILE), lambda b: (0, 0)),
        ],
        out_shape=[
            jax.ShapeDtypeStruct((16, 2, rows // TILE, 16, TILE), BF16),
            jax.ShapeDtypeStruct((8, TILE), F32),
        ],
        name="pack",
    )(gate_in, value_in, taps)


def unpack_kernel(data, *rest):
    out, signal, taps = rest[-3:]
    shards, _, blocks, channels, _ = data.shape
    rows = blocks * channels

    @pl.loop(0, shards)
    def _(a):
        part = pl.ds(pl.multiple_of(a * rows, rows), rows)
        signal[part, :] = data[a, 0].astype(F32).reshape(rows, TILE)
        taps[part, :] = data[a, 1].astype(F32).reshape(rows, TILE)

    for c in range(channels):
        pick = pl.ds(c, TILE, stride=channels)
        out[c] = jnp.concatenate([signal[pick, :], taps[pick, :]], 1).astype(BF16)


def unpack(data, after):
    shards, _, blocks, channels, _ = data.shape
    whole = pltpu.VMEM((shards * blocks * channels, TILE), F32)
    space = pl.BlockSpec(memory_space=pltpu.VMEM)
    return pl.pallas_call(
        unpack_kernel,
        in_specs=[space] + [pl.BlockSpec(memory_space=pl.ANY)] * len(after),
        out_specs=space,
        out_shape=jax.ShapeDtypeStruct((channels, TILE, 2 * TILE), BF16),
        scratch_shapes=[whole] * 2,
        compiler_params=pltpu.CompilerParams(vmem_limit_bytes=8 << 20),
        name="unpack",
    )(data, *after)


def conv_kernel(group, pairs, turns, twists, out, total):
    shards, blocks, channels, _ = out.shape
    rows = blocks * channels
    span = 2 * TILE
    first, second, back = turns.at[:span], turns.at[span : 4 * span], turns.at[4 * span : 7 * span]
    cosine, sine = twists.at[:TILE], twists.at[TILE:]
    last = [turns[7 * span + k * TILE : 7 * span + (k + 1) * TILE, :] for k in range(3)]

    @pl.loop(0, channels // group)
    def _(step):
        cos, sin = cosine[...], sine[...]
        picks = [pl.ds(step * group + g, TILE, stride=channels) for g in range(group)]
        pieces = []
        for g in range(group):
            pair = pairs[step * group + g]
            lifted = matmul(first[...], jnp.concatenate([pair, pair], 0))
            for side in range(2):
                real = lifted[:TILE, side * TILE : (side + 1) * TILE]
                imag = lifted[TILE:, side * TILE : (side + 1) * TILE]
                turned = jnp.concatenate([real * cos + imag * sin, imag * cos - real * sin], 1)
                high, low = halves(turned)
                pieces.append(jnp.concatenate([high, low, high], 1))
        spectra = matmul(jnp.concatenate(pieces, 0), second[...])
        pieces = []
        for g in range(group):
            left = spectra[2 * g * TILE : (2 * g + 1) * TILE]
            right = spectra[(2 * g + 1) * TILE : (2 * g + 2) * TILE]
            real = left[:, :TILE] * right[:, :TILE] - left[:, TILE:] * right[:, TILE:]
            imag = left[:, :TILE] * right[:, TILE:] + left[:, TILE:] * right[:, :TILE]
            high, low = halves(jnp.concatenate([real, imag], 1))
            pieces.append(jnp.concatenate([high, low, high], 1))
        restored = matmul(jnp.concatenate(pieces, 0), back[...])
        pieces = []
        for g in range(group):
            real = restored[g * TILE : (g + 1) * TILE, :TILE]
            imag = restored[g * TILE : (g + 1) * TILE, TILE:]
            turned = jnp.concatenate([real * cos - imag * sin, imag * cos + real * sin], 0)
            high, low = halves(turned)
            pieces.append(jnp.concatenate([high, low, high], 0))
        result = matmul(jnp.concatenate(last, 1), jnp.concatenate(pieces, 1))
        for g, pick in enumerate(picks):
            total[pick, :] = result[:, g * TILE : (g + 1) * TILE]

    @pl.loop(0, shards)
    def _(a):
        part = pl.ds(pl.multiple_of(a * rows, rows), rows)
        out[a] = total[part, :].astype(BF16).reshape(blocks, channels, TILE)


def convolve(pairs, blocks, group=8):
    channels, rows, _ = pairs.shape
    space = pl.BlockSpec(memory_space=pltpu.VMEM)
    return pl.pallas_call(
        functools.partial(conv_kernel, group),
        in_specs=[space] * 3,
        out_specs=space,
        out_shape=jax.ShapeDtypeStruct((rows // blocks, blocks, channels, TILE), BF16),
        scratch_shapes=[pltpu.VMEM((rows * channels, TILE), F32)],
        compiler_params=pltpu.CompilerParams(vmem_limit_bytes=28 << 20),
        cost_estimate=pl.CostEstimate(flops=10**10, bytes_accessed=1 << 22, transcendentals=0),
        name="convolve",
    )(pairs, *(jnp.asarray(table) for table in tables()))


def mix_kernel(start, conv, gate_out, gate_in, value_in, skip, _, top, low):
    rows = gate_out.shape[0]
    step = pl.program_id(0)
    shard = lax.axis_index("seq") * (rows * pl.num_programs(0))

    def fill(out):
        for b in range(rows // TILE):
            part = slice(b * TILE, (b + 1) * TILE)
            first = shard + step * rows + b * TILE
            position = first + lax.broadcasted_iota(jnp.int32, (TILE, 1), 0)
            signal = gate_in[part].astype(F32) * value_in[part].astype(F32)
            convolved = conv[:, b].reshape(-1, TILE).T.astype(F32)
            mixed = gate_out[part].astype(F32) * (convolved + skip[...] * signal)
            out[part] = jnp.where(position >= start[0], mixed, 0.0).astype(BF16)

    @pl.when(step == 0)
    def _():
        fill(top)

    @pl.when(step == 1)
    def _():
        fill(low)


def mix(resume_at, conv, gate_out, gate_in, value_in, skip_bias, after):
    rows, channels = value_in.shape
    half = rows // 2
    block = pl.BlockSpec((half, channels), lambda i: (i, 0))
    kept = pl.BlockSpec((half, channels), lambda i: (0, 0))
    return pl.pallas_call(
        mix_kernel,
        grid=(2,),
        in_specs=[
            pl.BlockSpec(memory_space=pltpu.SMEM),
            pl.BlockSpec((16, half // TILE, 16, TILE), lambda i: (0, i, 0, 0)),
            block,
            block,
            block,
            pl.BlockSpec((1, channels), lambda i: (0, 0)),
            pl.BlockSpec(memory_space=pl.ANY),
        ],
        out_specs=[kept] * 2,
        out_shape=[jax.ShapeDtypeStruct((half, channels), BF16)] * 2,
        compiler_params=pltpu.CompilerParams(vmem_limit_bytes=12 << 20),
        name="mix",
    )(resume_at, conv, gate_out, gate_in, value_in, skip_bias[None, :], after)


def toward(array, step, swap):
    pairs = [(z * 2 + c, (z + step) % 4 * 2 + (c ^ swap)) for z in range(4) for c in range(2)]
    return lax.ppermute(array, "chan", pairs)


ROUTES = ((1, 0), (3, 0), (1, 1), (3, 1), (2, 0), (2, 1), (0, 1), (0, 0))


def split_kernel(weight, _, *outs):
    me = lax.axis_index("chan")
    features = outs[0].shape[1]
    core = lax.rem(me, 2)
    for out, (step, swap) in zip(outs, ROUTES):
        target = lax.rem(me // 2 + step, 4) * 2 + (1 - core if swap else core)
        out[...] = weight[:, pl.ds(pl.multiple_of(target * features, features), features)]


def split_weight(weight, after, tile=128):
    channels, features = weight.shape
    members = len(ROUTES)
    width = features // members
    return pl.pallas_call(
        split_kernel,
        grid=(channels // tile,),
        in_specs=[
            pl.BlockSpec((tile, features), lambda i: (i, 0)),
            pl.BlockSpec(memory_space=pl.ANY),
        ],
        out_specs=[pl.BlockSpec((tile, width), lambda i: (i, 0))] * members,
        out_shape=[jax.ShapeDtypeStruct((channels, width), BF16)] * members,
        compiler_params=pltpu.CompilerParams(vmem_limit_bytes=12 << 20),
        name="split_weight",
    )(weight, after)


def mark_kernel(*refs):
    refs[-1][...] = jnp.zeros_like(refs[-1])


def mark(arrays):
    return pl.pallas_call(
        mark_kernel,
        in_specs=[pl.BlockSpec(memory_space=pl.ANY)] * len(arrays),
        out_shape=jax.ShapeDtypeStruct((8, TILE), F32),
        compiler_params=pltpu.CompilerParams(vmem_limit_bytes=2 << 20),
        cost_estimate=pl.CostEstimate(flops=10**10, bytes_accessed=0, transcendentals=0),
        name="mark",
    )(*arrays)


def fold_kernel(*refs):
    top, low, weight = refs[:4], refs[4:8], refs[8:13]
    partial, first, second = refs[13:]
    rows = top[0].shape[0]
    for half, pieces in enumerate((top, low)):
        total = None
        for piece, k in zip(pieces, ((0, 1, 2, 3), (0, 3, 4, 1))[half]):
            term = matmul(piece[...], weight[k][...])
            total = term if total is None else total + term
        partial[half * rows : half * rows + rows] = total
    first[...] = top[3][...]
    second[...] = low[3][...]


def fold(top, low, weight):
    rows = top[0].shape[0]
    features = weight[0].shape[1]
    space = pl.BlockSpec(memory_space=pltpu.VMEM)
    piece = jax.ShapeDtypeStruct(top[0].shape, BF16)
    return pl.pallas_call(
        fold_kernel,
        in_specs=[space] * 13,
        out_specs=[space] * 3,
        out_shape=[jax.ShapeDtypeStruct((2 * rows, features), F32), piece, piece],
        compiler_params=pltpu.CompilerParams(vmem_limit_bytes=12 << 20),
        cost_estimate=pl.CostEstimate(flops=0, bytes_accessed=0, transcendentals=0),
        name="fold",
    )(*top, *low, *weight)


def project_kernel(*refs):
    mixed, weight, partial, out = refs[:8], refs[8:13], refs[13], refs[14]
    rows = out.shape[0]

    def fill(half):
        total = partial[half * rows : half * rows + rows]
        places = ((0, 1, 2, 3), (0, 1, 2, 4))[half]
        for piece, k in zip(mixed[4 * half : 4 * half + 4], places):
            total = total + matmul(piece[...], weight[k][...])
        out[...] = total.astype(BF16)

    for half in range(2):
        pl.when(pl.program_id(0) == half)(functools.partial(fill, half))


def project(top, low, weight, partial):
    rows = top[0].shape[0]
    features = weight[0].shape[1]
    return pl.pallas_call(
        project_kernel,
        grid=(2,),
        in_specs=[pl.BlockSpec(memory_space=pltpu.VMEM)] * 14,
        out_specs=pl.BlockSpec((rows, features), lambda i: (i, 0)),
        out_shape=jax.ShapeDtypeStruct((2 * rows, features), BF16),
        compiler_params=pltpu.CompilerParams(vmem_limit_bytes=12 << 20),
        name="project",
    )(*top, *low, *weight, partial)


def on_device(gate_out, gate_in, value_in, filter_taps, skip_bias, resume_at, out_weight):
    packed, token = pack(gate_in, value_in, filter_taps)
    data = lax.all_to_all(packed, "seq", split_axis=0, concat_axis=0, tiled=True)
    weight = split_weight(out_weight, token)
    weight = [toward(w, *route) if any(route) else w for w, route in zip(weight, ROUTES)]
    conv = lax.all_to_all(convolve(unpack(data, weight[:2]), packed.shape[2]), "seq", split_axis=0, concat_axis=0, tiled=True)
    top, low = mix(resume_at, conv, gate_out, gate_in, value_in, skip_bias, mark(weight))
    up_top, down_low = toward(top, 1, 0), toward(low, 3, 0)
    up_low, down_top = toward(low, 1, 0), toward(top, 3, 0)
    far_top, far_low = toward(up_top, 1, 0), toward(down_low, 3, 0)
    up_top_other, down_low_other = toward(up_top, 0, 1), toward(down_low, 0, 1)
    weight = {route: weight[ROUTES.index(route)] for route in ROUTES}
    factors = [weight[route] for route in ((0, 0), (1, 0), (1, 1), (3, 0), (3, 1))]
    partial, down_top, up_low = fold(
        [top, up_top, up_top_other, down_top], [low, down_low, down_low_other, up_low], factors
    )
    tops = [toward(top, 0, 1), far_top, toward(far_top, 0, 1), toward(down_top, 0, 1)]
    lows = [toward(low, 0, 1), far_low, toward(far_low, 0, 1), toward(up_low, 0, 1)]
    factors = [weight[route] for route in ((0, 1), (2, 0), (2, 1), (3, 1), (1, 1))]
    return project(tops, lows, factors, partial)


def solution(mesh):
    placed = (
        P("seq", "chan"),
        P("seq", "chan"),
        P("seq", "chan"),
        P("seq", "chan"),
        P("chan"),
        P(),
        P("chan", None),
    )
    return jax.shard_map(
        on_device, mesh=mesh, in_specs=placed, out_specs=P("seq", "chan"), check_vma=False
    )
```

```python
import functools
import math

import jax
import jax.numpy as jnp
import numpy as np
from jax import lax
from jax.experimental import pallas as pl
from jax.experimental.pallas import tpu as pltpu
from jax.sharding import PartitionSpec as P

BF16 = jnp.bfloat16
F32 = jnp.float32
TILE = 128
LENGTH = TILE * TILE


def split_table(table):
    high = table.astype(jnp.bfloat16)
    low = (table - high.astype(np.float64)).astype(jnp.bfloat16)
    return high, low


@functools.lru_cache(None)
def tables():
    index = np.arange(TILE, dtype=np.float64)
    outer = 2 * math.pi * np.outer(4 * index + 1, index)
    turn = outer / 512
    first = np.concatenate([np.cos(turn), -np.sin(turn)], 0)
    first_high, first_low = split_table(first)
    last_high, last_low = split_table(first.T / LENGTH)
    twist = outer / (4 * LENGTH)
    angle = 2 * math.pi * np.outer(index, index) / TILE
    cosine, sine = np.cos(angle), np.sin(angle)
    second = np.block([[cosine, -sine], [sine, cosine]])
    second_high, second_low = split_table(second)
    back_high, back_low = split_table(second.T)
    turns = np.concatenate(
        [
            np.concatenate([first_high, first_low], 1),
            second_high,
            second_high,
            second_low,
            back_high,
            back_high,
            back_low,
            last_high,
            last_high,
            last_low,
        ],
        0,
    )
    twists = np.concatenate([np.cos(twist), np.sin(twist)], 0).astype(np.float32)
    return turns, twists


def halves(array):
    high = array.astype(BF16)
    return high, (array - high.astype(F32)).astype(BF16)


def matmul(left, right):
    return jnp.dot(left, right, preferred_element_type=F32)


def pack_kernel(gate_in, value_in, taps, out, token):
    token[...] = jnp.zeros_like(token)
    for b in range(out.shape[2]):
        rows = slice(b * TILE, (b + 1) * TILE)
        signal = gate_in[rows].astype(F32) * value_in[rows].astype(F32)
        out[:, 0, b] = signal.astype(BF16).T.reshape(16, 16, TILE)
        out[:, 1, b] = taps[rows].astype(BF16).T.reshape(16, 16, TILE)


def pack(gate_in, value_in, taps, blocks=4):
    rows, channels = value_in.shape
    block = pl.BlockSpec((blocks * TILE, channels), lambda b: (b, 0))
    return pl.pallas_call(
        pack_kernel,
        grid=(rows // (blocks * TILE),),
        in_specs=[block] * 3,
        out_specs=[
            pl.BlockSpec((16, 2, blocks, 16, TILE), lambda b: (0, 0, b, 0, 0)),
            pl.BlockSpec((8, TILE), lambda b: (0, 0)),
        ],
        out_shape=[
            jax.ShapeDtypeStruct((16, 2, rows // TILE, 16, TILE), BF16),
            jax.ShapeDtypeStruct((8, TILE), F32),
        ],
        name="pack",
    )(gate_in, value_in, taps)


def unpack_kernel(data, *rest):
    out, signal, taps = rest[-3:]
    shards, _, blocks, channels, _ = data.shape
    rows = blocks * channels

    @pl.loop(0, shards)
    def _(a):
        part = pl.ds(pl.multiple_of(a * rows, rows), rows)
        signal[part, :] = data[a, 0].astype(F32).reshape(rows, TILE)
        taps[part, :] = data[a, 1].astype(F32).reshape(rows, TILE)

    for c in range(channels):
        pick = pl.ds(c, TILE, stride=channels)
        out[c] = jnp.concatenate([signal[pick, :], taps[pick, :]], 1).astype(BF16)


def unpack(data, after):
    shards, _, blocks, channels, _ = data.shape
    whole = pltpu.VMEM((shards * blocks * channels, TILE), F32)
    space = pl.BlockSpec(memory_space=pltpu.VMEM)
    return pl.pallas_call(
        unpack_kernel,
        in_specs=[space] + [pl.BlockSpec(memory_space=pl.ANY)] * len(after),
        out_specs=space,
        out_shape=jax.ShapeDtypeStruct((channels, TILE, 2 * TILE), BF16),
        scratch_shapes=[whole] * 2,
        compiler_params=pltpu.CompilerParams(vmem_limit_bytes=8 << 20),
        name="unpack",
    )(data, *after)


def conv_kernel(group, pairs, turns, twists, out, total):
    shards, blocks, channels, _ = out.shape
    rows = blocks * channels
    span = 2 * TILE
    first, second, back = turns.at[:span], turns.at[span : 4 * span], turns.at[4 * span : 7 * span]
    cosine, sine = twists.at[:TILE], twists.at[TILE:]
    last = [turns[7 * span + k * TILE : 7 * span + (k + 1) * TILE, :] for k in range(3)]

    @pl.loop(0, channels // group)
    def _(step):
        cos, sin = cosine[...], sine[...]
        picks = [pl.ds(step * group + g, TILE, stride=channels) for g in range(group)]
        pieces = []
        for g in range(group):
            pair = pairs[step * group + g]
            lifted = matmul(first[...], jnp.concatenate([pair, pair], 0))
            for side in range(2):
                real = lifted[:TILE, side * TILE : (side + 1) * TILE]
                imag = lifted[TILE:, side * TILE : (side + 1) * TILE]
                turned = jnp.concatenate([real * cos + imag * sin, imag * cos - real * sin], 1)
                high, low = halves(turned)
                pieces.append(jnp.concatenate([high, low, high], 1))
        spectra = matmul(jnp.concatenate(pieces, 0), second[...])
        pieces = []
        for g in range(group):
            left = spectra[2 * g * TILE : (2 * g + 1) * TILE]
            right = spectra[(2 * g + 1) * TILE : (2 * g + 2) * TILE]
            real = left[:, :TILE] * right[:, :TILE] - left[:, TILE:] * right[:, TILE:]
            imag = left[:, :TILE] * right[:, TILE:] + left[:, TILE:] * right[:, :TILE]
            high, low = halves(jnp.concatenate([real, imag], 1))
            pieces.append(jnp.concatenate([high, low, high], 1))
        restored = matmul(jnp.concatenate(pieces, 0), back[...])
        pieces = []
        for g in range(group):
            real = restored[g * TILE : (g + 1) * TILE, :TILE]
            imag = restored[g * TILE : (g + 1) * TILE, TILE:]
            turned = jnp.concatenate([real * cos - imag * sin, imag * cos + real * sin], 0)
            high, low = halves(turned)
            pieces.append(jnp.concatenate([high, low, high], 0))
        result = matmul(jnp.concatenate(last, 1), jnp.concatenate(pieces, 1))
        for g, pick in enumerate(picks):
            total[pick, :] = result[:, g * TILE : (g + 1) * TILE]

    @pl.loop(0, shards)
    def _(a):
        part = pl.ds(pl.multiple_of(a * rows, rows), rows)
        out[a] = total[part, :].astype(BF16).reshape(blocks, channels, TILE)


def convolve(pairs, blocks, group=16):
    channels, rows, _ = pairs.shape
    space = pl.BlockSpec(memory_space=pltpu.VMEM)
    return pl.pallas_call(
        functools.partial(conv_kernel, group),
        in_specs=[space] * 3,
        out_specs=space,
        out_shape=jax.ShapeDtypeStruct((rows // blocks, blocks, channels, TILE), BF16),
        scratch_shapes=[pltpu.VMEM((rows * channels, TILE), F32)],
        compiler_params=pltpu.CompilerParams(vmem_limit_bytes=28 << 20),
        cost_estimate=pl.CostEstimate(flops=10**10, bytes_accessed=1 << 22, transcendentals=0),
        name="convolve",
    )(pairs, *(jnp.asarray(table) for table in tables()))


def mix_kernel(start, conv, gate_out, gate_in, value_in, skip, _, top, low):
    rows = gate_out.shape[0]
    step = pl.program_id(0)
    shard = lax.axis_index("seq") * (rows * pl.num_programs(0))

    def fill(out):
        for b in range(rows // TILE):
            part = slice(b * TILE, (b + 1) * TILE)
            first = shard + step * rows + b * TILE
            position = first + lax.broadcasted_iota(jnp.int32, (TILE, 1), 0)
            signal = gate_in[part].astype(F32) * value_in[part].astype(F32)
            convolved = conv[:, b].reshape(-1, TILE).T.astype(F32)
            mixed = gate_out[part].astype(F32) * (convolved + skip[...] * signal)
            out[part] = jnp.where(position >= start[0], mixed, 0.0).astype(BF16)

    @pl.when(step == 0)
    def _():
        fill(top)

    @pl.when(step == 1)
    def _():
        fill(low)


def mix(resume_at, conv, gate_out, gate_in, value_in, skip_bias, after):
    rows, channels = value_in.shape
    half = rows // 2
    block = pl.BlockSpec((half, channels), lambda i: (i, 0))
    kept = pl.BlockSpec((half, channels), lambda i: (0, 0))
    return pl.pallas_call(
        mix_kernel,
        grid=(2,),
        in_specs=[
            pl.BlockSpec(memory_space=pltpu.SMEM),
            pl.BlockSpec((16, half // TILE, 16, TILE), lambda i: (0, i, 0, 0)),
            block,
            block,
            block,
            pl.BlockSpec((1, channels), lambda i: (0, 0)),
            pl.BlockSpec(memory_space=pl.ANY),
        ],
        out_specs=[kept] * 2,
        out_shape=[jax.ShapeDtypeStruct((half, channels), BF16)] * 2,
        compiler_params=pltpu.CompilerParams(vmem_limit_bytes=12 << 20),
        name="mix",
    )(resume_at, conv, gate_out, gate_in, value_in, skip_bias[None, :], after)


def toward(array, step, swap):
    pairs = [(z * 2 + c, (z + step) % 4 * 2 + (c ^ swap)) for z in range(4) for c in range(2)]
    return lax.ppermute(array, "chan", pairs)


ROUTES = ((1, 0), (3, 0), (1, 1), (3, 1), (2, 0), (2, 1), (0, 1), (0, 0))


def split_kernel(weight, _, *outs):
    me = lax.axis_index("chan")
    features = outs[0].shape[1]
    core = lax.rem(me, 2)
    for out, (step, swap) in zip(outs, ROUTES):
        target = lax.rem(me // 2 + step, 4) * 2 + (1 - core if swap else core)
        out[...] = weight[:, pl.ds(pl.multiple_of(target * features, features), features)]


def split_weight(weight, after, tile=128):
    channels, features = weight.shape
    members = len(ROUTES)
    width = features // members
    return pl.pallas_call(
        split_kernel,
        grid=(channels // tile,),
        in_specs=[
            pl.BlockSpec((tile, features), lambda i: (i, 0)),
            pl.BlockSpec(memory_space=pl.ANY),
        ],
        out_specs=[pl.BlockSpec((tile, width), lambda i: (i, 0))] * members,
        out_shape=[jax.ShapeDtypeStruct((channels, width), BF16)] * members,
        compiler_params=pltpu.CompilerParams(vmem_limit_bytes=12 << 20),
        name="split_weight",
    )(weight, after)


def mark_kernel(*refs):
    refs[-1][...] = jnp.zeros_like(refs[-1])


def mark(arrays):
    return pl.pallas_call(
        mark_kernel,
        in_specs=[pl.BlockSpec(memory_space=pl.ANY)] * len(arrays),
        out_shape=jax.ShapeDtypeStruct((8, TILE), F32),
        compiler_params=pltpu.CompilerParams(vmem_limit_bytes=2 << 20),
        cost_estimate=pl.CostEstimate(flops=10**10, bytes_accessed=0, transcendentals=0),
        name="mark",
    )(*arrays)


def fold_kernel(*refs):
    top, low, weight = refs[:4], refs[4:8], refs[8:13]
    partial, first, second = refs[13:]
    rows = top[0].shape[0]
    for half, pieces in enumerate((top, low)):
        total = None
        for piece, k in zip(pieces, ((0, 1, 2, 3), (0, 3, 4, 1))[half]):
            term = matmul(piece[...], weight[k][...])
            total = term if total is None else total + term
        partial[half * rows : half * rows + rows] = total
    first[...] = top[3][...]
    second[...] = low[3][...]


def fold(top, low, weight):
    rows = top[0].shape[0]
    features = weight[0].shape[1]
    space = pl.BlockSpec(memory_space=pltpu.VMEM)
    piece = jax.ShapeDtypeStruct(top[0].shape, BF16)
    return pl.pallas_call(
        fold_kernel,
        in_specs=[space] * 13,
        out_specs=[space] * 3,
        out_shape=[jax.ShapeDtypeStruct((2 * rows, features), F32), piece, piece],
        compiler_params=pltpu.CompilerParams(vmem_limit_bytes=12 << 20),
        cost_estimate=pl.CostEstimate(flops=0, bytes_accessed=0, transcendentals=0),
        name="fold",
    )(*top, *low, *weight)


def project_kernel(*refs):
    mixed, weight, partial, out = refs[:8], refs[8:13], refs[13], refs[14]
    rows = out.shape[0]

    def fill(half):
        total = partial[half * rows : half * rows + rows]
        places = ((0, 1, 2, 3), (0, 1, 2, 4))[half]
        for piece, k in zip(mixed[4 * half : 4 * half + 4], places):
            total = total + matmul(piece[...], weight[k][...])
        out[...] = total.astype(BF16)

    for half in range(2):
        pl.when(pl.program_id(0) == half)(functools.partial(fill, half))


def project(top, low, weight, partial):
    rows = top[0].shape[0]
    features = weight[0].shape[1]
    return pl.pallas_call(
        project_kernel,
        grid=(2,),
        in_specs=[pl.BlockSpec(memory_space=pltpu.VMEM)] * 14,
        out_specs=pl.BlockSpec((rows, features), lambda i: (i, 0)),
        out_shape=jax.ShapeDtypeStruct((2 * rows, features), BF16),
        compiler_params=pltpu.CompilerParams(vmem_limit_bytes=12 << 20),
        name="project",
    )(*top, *low, *weight, partial)


def on_device(gate_out, gate_in, value_in, filter_taps, skip_bias, resume_at, out_weight):
    packed, token = pack(gate_in, value_in, filter_taps)
    data = lax.all_to_all(packed, "seq", split_axis=0, concat_axis=0, tiled=True)
    weight = split_weight(out_weight, token)
    weight = [toward(w, *route) if any(route) else w for w, route in zip(weight, ROUTES)]
    conv = lax.all_to_all(convolve(unpack(data, weight[:2]), packed.shape[2]), "seq", split_axis=0, concat_axis=0, tiled=True)
    top, low = mix(resume_at, conv, gate_out, gate_in, value_in, skip_bias, mark(weight))
    up_top, down_low = toward(top, 1, 0), toward(low, 3, 0)
    up_low, down_top = toward(low, 1, 0), toward(top, 3, 0)
    far_top, far_low = toward(up_top, 1, 0), toward(down_low, 3, 0)
    up_top_other, down_low_other = toward(up_top, 0, 1), toward(down_low, 0, 1)
    weight = {route: weight[ROUTES.index(route)] for route in ROUTES}
    factors = [weight[route] for route in ((0, 0), (1, 0), (1, 1), (3, 0), (3, 1))]
    partial, down_top, up_low = fold(
        [top, up_top, up_top_other, down_top], [low, down_low, down_low_other, up_low], factors
    )
    tops = [toward(top, 0, 1), far_top, toward(far_top, 0, 1), toward(down_top, 0, 1)]
    lows = [toward(low, 0, 1), far_low, toward(far_low, 0, 1), toward(up_low, 0, 1)]
    factors = [weight[route] for route in ((0, 1), (2, 0), (2, 1), (3, 1), (1, 1))]
    return project(tops, lows, factors, partial)


def solution(mesh):
    placed = (
        P("seq", "chan"),
        P("seq", "chan"),
        P("seq", "chan"),
        P("seq", "chan"),
        P("chan"),
        P(),
        P("chan", None),
    )
    return jax.shard_map(
        on_device, mesh=mesh, in_specs=placed, out_specs=P("seq", "chan"), check_vma=False
    )
```

```python
import functools
import math

import jax
import jax.numpy as jnp
import numpy as np
from jax import lax
from jax.experimental import pallas as pl
from jax.experimental.pallas import tpu as pltpu
from jax.sharding import PartitionSpec as P

BF16 = jnp.bfloat16
F32 = jnp.float32
TILE = 128
LENGTH = TILE * TILE


def split_table(table):
    high = table.astype(jnp.bfloat16)
    low = (table - high.astype(np.float64)).astype(jnp.bfloat16)
    return high, low


@functools.lru_cache(None)
def tables():
    index = np.arange(TILE, dtype=np.float64)
    outer = 2 * math.pi * np.outer(4 * index + 1, index)
    turn = outer / 512
    first = np.concatenate([np.cos(turn), -np.sin(turn)], 0)
    first_high, first_low = split_table(first)
    last_high, last_low = split_table(first.T / LENGTH)
    twist = outer / (4 * LENGTH)
    angle = 2 * math.pi * np.outer(index, index) / TILE
    cosine, sine = np.cos(angle), np.sin(angle)
    second = np.block([[cosine, -sine], [sine, cosine]])
    second_high, second_low = split_table(second)
    back_high, back_low = split_table(second.T)
    turns = np.concatenate(
        [
            np.concatenate([first_high, first_low], 1),
            second_high,
            second_high,
            second_low,
            back_high,
            back_high,
            back_low,
            last_high,
            last_high,
            last_low,
        ],
        0,
    )
    twists = np.concatenate([np.cos(twist), np.sin(twist)], 0).astype(np.float32)
    return turns, twists


def halves(array):
    high = array.astype(BF16)
    return high, (array - high.astype(F32)).astype(BF16)


def matmul(left, right):
    return jnp.dot(left, right, preferred_element_type=F32)


def pack_kernel(gate_in, value_in, taps, out, token):
    token[...] = jnp.zeros_like(token)
    for b in range(out.shape[2]):
        rows = slice(b * TILE, (b + 1) * TILE)
        signal = gate_in[rows].astype(F32) * value_in[rows].astype(F32)
        out[:, 0, b] = signal.astype(BF16).T.reshape(16, 16, TILE)
        out[:, 1, b] = taps[rows].astype(BF16).T.reshape(16, 16, TILE)


def pack(gate_in, value_in, taps, blocks=4):
    rows, channels = value_in.shape
    block = pl.BlockSpec((blocks * TILE, channels), lambda b: (b, 0))
    return pl.pallas_call(
        pack_kernel,
        grid=(rows // (blocks * TILE),),
        in_specs=[block] * 3,
        out_specs=[
            pl.BlockSpec((16, 2, blocks, 16, TILE), lambda b: (0, 0, b, 0, 0)),
            pl.BlockSpec((8, TILE), lambda b: (0, 0)),
        ],
        out_shape=[
            jax.ShapeDtypeStruct((16, 2, rows // TILE, 16, TILE), BF16),
            jax.ShapeDtypeStruct((8, TILE), F32),
        ],
        name="pack",
    )(gate_in, value_in, taps)


def unpack_kernel(data, *rest):
    out, signal, taps = rest[-3:]
    shards, _, blocks, channels, _ = data.shape
    rows = blocks * channels

    @pl.loop(0, shards)
    def _(a):
        part = pl.ds(pl.multiple_of(a * rows, rows), rows)
        signal[part, :] = data[a, 0].astype(F32).reshape(rows, TILE)
        taps[part, :] = data[a, 1].astype(F32).reshape(rows, TILE)

    for c in range(channels):
        pick = pl.ds(c, TILE, stride=channels)
        out[c] = jnp.concatenate([signal[pick, :], taps[pick, :]], 1).astype(BF16)


def unpack(data, after):
    shards, _, blocks, channels, _ = data.shape
    whole = pltpu.VMEM((shards * blocks * channels, TILE), F32)
    space = pl.BlockSpec(memory_space=pltpu.VMEM)
    return pl.pallas_call(
        unpack_kernel,
        in_specs=[space] + [pl.BlockSpec(memory_space=pl.ANY)] * len(after),
        out_specs=space,
        out_shape=jax.ShapeDtypeStruct((channels, TILE, 2 * TILE), BF16),
        scratch_shapes=[whole] * 2,
        compiler_params=pltpu.CompilerParams(vmem_limit_bytes=8 << 20),
        name="unpack",
    )(data, *after)


def conv_kernel(group, pairs, turns, twists, out, total):
    shards, blocks, channels, _ = out.shape
    rows = blocks * channels
    span = 2 * TILE
    first, second, back = turns.at[:span], turns.at[span : 4 * span], turns.at[4 * span : 7 * span]
    cosine, sine = twists.at[:TILE], twists.at[TILE:]
    last = [turns[7 * span + k * TILE : 7 * span + (k + 1) * TILE, :] for k in range(3)]

    @pl.loop(0, channels // group)
    def _(step):
        cos, sin = cosine[...], sine[...]
        picks = [pl.ds(step * group + g, TILE, stride=channels) for g in range(group)]
        pieces = []
        for g in range(group):
            pair = pairs[step * group + g]
            lifted = matmul(first[...], jnp.concatenate([pair, pair], 0))
            for side in range(2):
                real = lifted[:TILE, side * TILE : (side + 1) * TILE]
                imag = lifted[TILE:, side * TILE : (side + 1) * TILE]
                turned = jnp.concatenate([real * cos + imag * sin, imag * cos - real * sin], 1)
                high, low = halves(turned)
                pieces.append(jnp.concatenate([high, low, high], 1))
        spectra = matmul(jnp.concatenate(pieces, 0), second[...])
        pieces = []
        for g in range(group):
            left = spectra[2 * g * TILE : (2 * g + 1) * TILE]
            right = spectra[(2 * g + 1) * TILE : (2 * g + 2) * TILE]
            real = left[:, :TILE] * right[:, :TILE] - left[:, TILE:] * right[:, TILE:]
            imag = left[:, :TILE] * right[:, TILE:] + left[:, TILE:] * right[:, :TILE]
            high, low = halves(jnp.concatenate([real, imag], 1))
            pieces.append(jnp.concatenate([high, low, high], 1))
        restored = matmul(jnp.concatenate(pieces, 0), back[...])
        pieces = []
        for g in range(group):
            real = restored[g * TILE : (g + 1) * TILE, :TILE]
            imag = restored[g * TILE : (g + 1) * TILE, TILE:]
            turned = jnp.concatenate([real * cos - imag * sin, imag * cos + real * sin], 0)
            high, low = halves(turned)
            pieces.append(jnp.concatenate([high, low, high], 0))
        result = matmul(jnp.concatenate(last, 1), jnp.concatenate(pieces, 1))
        for g, pick in enumerate(picks):
            total[pick, :] = result[:, g * TILE : (g + 1) * TILE]

    @pl.loop(0, shards)
    def _(a):
        part = pl.ds(pl.multiple_of(a * rows, rows), rows)
        out[a] = total[part, :].astype(BF16).reshape(blocks, channels, TILE)


def convolve(pairs, blocks, group=8):
    channels, rows, _ = pairs.shape
    space = pl.BlockSpec(memory_space=pltpu.VMEM)
    return pl.pallas_call(
        functools.partial(conv_kernel, group),
        in_specs=[space] * 3,
        out_specs=space,
        out_shape=jax.ShapeDtypeStruct((rows // blocks, blocks, channels, TILE), BF16),
        scratch_shapes=[pltpu.VMEM((rows * channels, TILE), F32)],
        compiler_params=pltpu.CompilerParams(vmem_limit_bytes=28 << 20),
        cost_estimate=pl.CostEstimate(flops=10**10, bytes_accessed=1 << 22, transcendentals=0),
        name="convolve",
    )(pairs, *(jnp.asarray(table) for table in tables()))


def mix_kernel(start, conv, gate_out, gate_in, value_in, skip, _, top, low):
    rows = gate_out.shape[0]
    step = pl.program_id(0)
    shard = lax.axis_index("seq") * (rows * pl.num_programs(0))

    def fill(out):
        for b in range(rows // TILE):
            part = slice(b * TILE, (b + 1) * TILE)
            first = shard + step * rows + b * TILE
            position = first + lax.broadcasted_iota(jnp.int32, (TILE, 1), 0)
            signal = gate_in[part].astype(F32) * value_in[part].astype(F32)
            convolved = conv[:, b].reshape(-1, TILE).T.astype(F32)
            mixed = gate_out[part].astype(F32) * (convolved + skip[...] * signal)
            out[part] = jnp.where(position >= start[0], mixed, 0.0).astype(BF16)

    @pl.when(step == 0)
    def _():
        fill(top)

    @pl.when(step == 1)
    def _():
        fill(low)


def mix(resume_at, conv, gate_out, gate_in, value_in, skip_bias, after):
    rows, channels = value_in.shape
    half = rows // 2
    block = pl.BlockSpec((half, channels), lambda i: (i, 0))
    kept = pl.BlockSpec((half, channels), lambda i: (0, 0))
    return pl.pallas_call(
        mix_kernel,
        grid=(2,),
        in_specs=[
            pl.BlockSpec(memory_space=pltpu.SMEM),
            pl.BlockSpec((16, half // TILE, 16, TILE), lambda i: (0, i, 0, 0)),
            block,
            block,
            block,
            pl.BlockSpec((1, channels), lambda i: (0, 0)),
            pl.BlockSpec(memory_space=pl.ANY),
        ],
        out_specs=[kept] * 2,
        out_shape=[jax.ShapeDtypeStruct((half, channels), BF16)] * 2,
        compiler_params=pltpu.CompilerParams(vmem_limit_bytes=12 << 20),
        name="mix",
    )(resume_at, conv, gate_out, gate_in, value_in, skip_bias[None, :], after)


def toward(array, step, swap):
    pairs = [(z * 2 + c, (z + step) % 4 * 2 + (c ^ swap)) for z in range(4) for c in range(2)]
    return lax.ppermute(array, "chan", pairs)


ROUTES = ((1, 0), (3, 0), (1, 1), (3, 1), (2, 0), (2, 1), (0, 1), (0, 0))


def split_kernel(weight, _, *outs):
    me = lax.axis_index("chan")
    features = outs[0].shape[1]
    core = lax.rem(me, 2)
    for out, (step, swap) in zip(outs, ROUTES):
        target = lax.rem(me // 2 + step, 4) * 2 + (1 - core if swap else core)
        out[...] = weight[:, pl.ds(pl.multiple_of(target * features, features), features)]


def split_weight(weight, after, tile=128):
    channels, features = weight.shape
    members = len(ROUTES)
    width = features // members
    return pl.pallas_call(
        split_kernel,
        grid=(channels // tile,),
        in_specs=[
            pl.BlockSpec((tile, features), lambda i: (i, 0)),
            pl.BlockSpec(memory_space=pl.ANY),
        ],
        out_specs=[pl.BlockSpec((tile, width), lambda i: (i, 0))] * members,
        out_shape=[jax.ShapeDtypeStruct((channels, width), BF16)] * members,
        compiler_params=pltpu.CompilerParams(vmem_limit_bytes=12 << 20),
        name="split_weight",
    )(weight, after)


def mark_kernel(*refs):
    refs[-1][...] = jnp.zeros_like(refs[-1])


def mark(arrays):
    return pl.pallas_call(
        mark_kernel,
        in_specs=[pl.BlockSpec(memory_space=pl.ANY)] * len(arrays),
        out_shape=jax.ShapeDtypeStruct((8, TILE), F32),
        compiler_params=pltpu.CompilerParams(vmem_limit_bytes=2 << 20),
        cost_estimate=pl.CostEstimate(flops=10**10, bytes_accessed=0, transcendentals=0),
        name="mark",
    )(*arrays)


def fold_kernel(*refs):
    top, low, weight = refs[:4], refs[4:8], refs[8:13]
    partial, late = refs[13:]
    rows = top[0].shape[0]
    for half, pieces in enumerate((top, low)):
        total = None
        for piece, k in zip(pieces, ((0, 1, 2, 3), (0, 3, 4, 1))[half]):
            term = matmul(piece[...], weight[k][...])
            total = term if total is None else total + term
        partial[half * rows : half * rows + rows] = total
    late[:rows] = top[3][...]
    late[rows:] = low[3][...]


def fold(top, low, weight):
    rows = top[0].shape[0]
    features = weight[0].shape[1]
    space = pl.BlockSpec(memory_space=pltpu.VMEM)
    late = jax.ShapeDtypeStruct((2 * rows, top[0].shape[1]), BF16)
    return pl.pallas_call(
        fold_kernel,
        in_specs=[space] * 13,
        out_specs=[space] * 2,
        out_shape=[jax.ShapeDtypeStruct((2 * rows, features), F32), late],
        compiler_params=pltpu.CompilerParams(vmem_limit_bytes=12 << 20),
        cost_estimate=pl.CostEstimate(flops=0, bytes_accessed=0, transcendentals=0),
        name="fold",
    )(*top, *low, *weight)


def join_kernel(first, second, out):
    rows = first.shape[0]
    out[:rows] = first[...]
    out[rows:] = second[...]


def join(first, second):
    rows, channels = first.shape
    space = pl.BlockSpec(memory_space=pltpu.VMEM)
    return pl.pallas_call(
        join_kernel,
        in_specs=[space] * 2,
        out_specs=space,
        out_shape=jax.ShapeDtypeStruct((2 * rows, channels), BF16),
        compiler_params=pltpu.CompilerParams(vmem_limit_bytes=12 << 20),
        name="join",
    )(first, second)


def project_kernel(*refs):
    others, fars, (far_other, late_other) = refs[:2], refs[2:4], refs[4:6]
    weight, partial, out = refs[6:11], refs[11], refs[12]
    rows = out.shape[0]

    def fill(half):
        part = slice(half * rows, half * rows + rows)
        total = partial[part] + matmul(others[half][...], weight[0][...])
        total = total + matmul(fars[half][...], weight[1][...])
        total = total + matmul(far_other[part], weight[2][...])
        total = total + matmul(late_other[part], weight[3 + half][...])
        out[...] = total.astype(BF16)

    for half in range(2):
        pl.when(pl.program_id(0) == half)(functools.partial(fill, half))


def project(mixed, weight, partial):
    rows = mixed[0].shape[0]
    features = weight[0].shape[1]
    return pl.pallas_call(
        project_kernel,
        grid=(2,),
        in_specs=[pl.BlockSpec(memory_space=pltpu.VMEM)] * 12,
        out_specs=pl.BlockSpec((rows, features), lambda i: (i, 0)),
        out_shape=jax.ShapeDtypeStruct((2 * rows, features), BF16),
        compiler_params=pltpu.CompilerParams(vmem_limit_bytes=12 << 20),
        name="project",
    )(*mixed, *weight, partial)


def on_device(gate_out, gate_in, value_in, filter_taps, skip_bias, resume_at, out_weight):
    packed, token = pack(gate_in, value_in, filter_taps)
    data = lax.all_to_all(packed, "seq", split_axis=0, concat_axis=0, tiled=True)
    weight = split_weight(out_weight, token)
    weight = [toward(w, *route) if any(route) else w for w, route in zip(weight, ROUTES)]
    conv = lax.all_to_all(convolve(unpack(data, weight[:2]), packed.shape[2]), "seq", split_axis=0, concat_axis=0, tiled=True)
    top, low = mix(resume_at, conv, gate_out, gate_in, value_in, skip_bias, mark(weight))
    up_top, down_low = toward(top, 1, 0), toward(low, 3, 0)
    up_low, down_top = toward(low, 1, 0), toward(top, 3, 0)
    far_top, far_low = toward(up_top, 1, 0), toward(down_low, 3, 0)
    up_top_other, down_low_other = toward(up_top, 0, 1), toward(down_low, 0, 1)
    weight = {route: weight[ROUTES.index(route)] for route in ROUTES}
    factors = [weight[route] for route in ((0, 0), (1, 0), (1, 1), (3, 0), (3, 1))]
    partial, late = fold(
        [top, up_top, up_top_other, down_top], [low, down_low, down_low_other, up_low], factors
    )
    far_other = toward(join(far_top, far_low), 0, 1)
    mixed = [toward(top, 0, 1), toward(low, 0, 1), far_top, far_low, far_other, toward(late, 0, 1)]
    factors = [weight[route] for route in ((0, 1), (2, 0), (2, 1), (3, 1), (1, 1))]
    return project(mixed, factors, partial)


def solution(mesh):
    placed = (
        P("seq", "chan"),
        P("seq", "chan"),
        P("seq", "chan"),
        P("seq", "chan"),
        P("chan"),
        P(),
        P("chan", None),
    )
    return jax.shard_map(
        on_device, mesh=mesh, in_specs=placed, out_specs=P("seq", "chan"), check_vma=False
    )
```
